256 devices in a mesh: seq: 32 (over z, y_lo, core), head: 8 (over x, y_hi).
Axes of the slice: x: 4, y: 4 (y_hi: 2, y_lo: 2; y = y_hi * 2 + y_lo), z: 8, core: 2. Of those that a mesh axis runs over, the one named last changes fastest.
Arguments:
- queries: bfloat16 [2048, 8192], P('seq', 'head'), may hold values from -15 to 15
- cache_keys: bfloat16 [8, 32768, 128], P('head', 'seq'), may hold values from -6 to 6
- cache_values: bfloat16 [8, 32768, 128], P('head', 'seq'), may hold values from -6 to 6
- new_keys: bfloat16 [2048, 1024], P('seq', 'head'), may hold values from -9.5625 to 9.5625
- new_values: bfloat16 [2048, 1024], P('seq', 'head'), may hold values from -6 to 6
- cache_len: int32 [32], P('seq'), may hold values from 256 to 1024, as said below
- span_rank: int32 [2048], replicated, may hold values from 0 to 2047, each once
- out_weight: bfloat16 [8192, 8192], P('head', 'seq'), may hold values from -0.0625 to 0.0625
Outputs:
- projected: bfloat16 [2048, 8192], P('head', 'seq')
The draws below stay inside these ranges and needn't reach their ends.
Inputs may be any that keep to these rules, and one draw needn't show every extreme that they name: `cache_len`: each shard holds at least 256 filled positions; one shard is full in every draw.
All inputs are finite; a program needn't handle non-finite values.
Results may differ from the reference program's by a relative error of at most 0.006.
Values may be sent and summed in bfloat16 or wider, within the bound.
No kernel may reach another device: no remote copies, remote signals or barrier semaphores. Data moves between devices by JAX's collectives and lax.ppermute only.
A program may use at most 64 MiB of HBM per device.

```python
import math
import jax
import jax.numpy as jnp
from jax import lax

D = 8192
HD = 128
QPH = 8
KV_HEADS = 8
Q_HEADS = 64
SPAN_DEV = 64
SPAN = 2048
CACHE_DEV = 1024
SHARDS = 32
CONTEXT = 32768
BLOCK = 512


def draw_queries(key, part):
    key = jax.random.fold_in(key, 1)
    base = jnp.clip(2.5 * jax.random.normal(key, (SPAN, Q_HEADS, HD), jnp.float32), -15.0, 15.0)
    return base.reshape(SPAN, Q_HEADS * HD).astype(jnp.bfloat16)


def draw_cache_keys(key, part):
    key = jax.random.fold_in(key, 2)
    base = jnp.clip(jax.random.normal(key, (KV_HEADS, CONTEXT, HD), jnp.float32), -6.0, 6.0)
    return base.astype(jnp.bfloat16)


def draw_cache_len(key, part):
    key = jax.random.fold_in(key, 3)
    lengths = jax.random.randint(key, (SHARDS,), CACHE_DEV // 4, CACHE_DEV + 1)
    full_shard = jax.random.randint(jax.random.fold_in(key, 7), (), 0, SHARDS)
    return jnp.where(jnp.arange(SHARDS) == full_shard, CACHE_DEV, lengths).astype(jnp.int32)


def levels(key, shape, cuts, smallest, high):
    def one(dim, shards_of):
        steps = jax.random.uniform(jax.random.fold_in(jax.random.fold_in(key, 6), dim), (shards_of,), jnp.float32, smallest / len(cuts), high / len(cuts))
        return jnp.repeat(jnp.exp(steps), shape[dim] // shards_of).reshape((-1,) + (1,) * (len(shape) - dim - 1))

    level = one(*cuts[0])
    for cut in cuts[1:]:
        level = level * one(*cut)
    return level


def gaussian(own_key, extent, deviation, most, shards=(), held_as=jnp.bfloat16):
    loudness = levels(own_key, extent, shards, -0.22, 0.18) if shards else 1.0
    array = jax.random.normal(own_key, extent, jnp.float32) * deviation * loudness
    return jnp.minimum(jnp.maximum(array, -most), most).astype(held_as)


def setup_inputs(seed: int = 0) -> dict:
    arg_keys = jax.random.split(jax.random.key(seed), 9)
    queries = draw_queries(jax.random.fold_in(arg_keys[8], 71), 0)
    cache_keys = draw_cache_keys(jax.random.fold_in(arg_keys[8], 71), 0)
    cache_values = gaussian(arg_keys[2], (KV_HEADS, CONTEXT, HD), 1.0, 6.0, ((0, 8), (1, 32)))
    new_keys = gaussian(arg_keys[3], (SPAN, KV_HEADS * HD), 1.6, 9.5625, ((0, 32), (1, 8)))
    new_values = gaussian(arg_keys[4], (SPAN, KV_HEADS * HD), 1.0, 6.0, ((0, 32), (1, 8)))
    cache_len = draw_cache_len(jax.random.fold_in(arg_keys[8], 71), 0)
    span_rank = jax.random.permutation(arg_keys[6], SPAN).astype(jnp.int32)
    out_weight = gaussian(arg_keys[7], (Q_HEADS * HD, D), (Q_HEADS * HD) ** -0.5, 0.0625, ((0, 8), (1, 32)))
    return dict(queries=queries, cache_keys=cache_keys, cache_values=cache_values, new_keys=new_keys, new_values=new_values, cache_len=cache_len, span_rank=span_rank, out_weight=out_weight)


NEG_FILL = -1e+30

def combine(earlier, latter):
    sum_a, max_a, tot_a = earlier
    sum_b, max_b, tot_b = latter
    overall = jnp.maximum(max_a, max_b)
    factor_a = jnp.exp(max_a - overall)
    factor_b = jnp.exp(max_b - overall)
    return (sum_a * factor_a[..., None] + sum_b * factor_b[..., None], overall, tot_a * factor_a + tot_b * factor_b)

def block_terms(query_rows, key_rows, value_rows, usable, score_scale):
    scores = jnp.dot(query_rows, key_rows.T, preferred_element_type=jnp.float32) * score_scale
    scores = jnp.where(usable, scores, NEG_FILL)
    row_max = lax.optimization_barrier(jnp.max(scores, axis=1))
    weights = jnp.where(usable, jnp.exp(scores - row_max[:, None]), 0.0).astype(jnp.bfloat16)
    row_sum = lax.optimization_barrier(jnp.sum(weights.astype(jnp.float32), axis=1))
    summed = jnp.dot(weights, value_rows, preferred_element_type=jnp.float32)
    return (summed, row_max, row_sum)

def reference(queries, cache_keys, cache_values, new_keys, new_values, cache_len, span_rank, out_weight):
    score_scale = jnp.float32(1.0 / math.sqrt(HD))
    row_total = SPAN * QPH
    blocks = CACHE_DEV // BLOCK
    rank_rows = jnp.repeat(span_rank, QPH)
    shard_rank = span_rank.reshape(SHARDS, SPAN_DEV)
    positions = jnp.arange(CACHE_DEV, dtype=jnp.int32)
    pieces = []
    for kv_head in range(KV_HEADS):
        query_rows = queries[:, kv_head * QPH * HD:(kv_head + 1) * QPH * HD].reshape(row_total, HD)
        shard_keys = cache_keys[kv_head].reshape(SHARDS, CACHE_DEV, HD)
        shard_values = cache_values[kv_head].reshape(SHARDS, CACHE_DEV, HD)
        span_keys = new_keys[:, kv_head * HD:(kv_head + 1) * HD].reshape(SHARDS, SPAN_DEV, HD)
        span_values = new_values[:, kv_head * HD:(kv_head + 1) * HD].reshape(SHARDS, SPAN_DEV, HD)

        def visit(running, inputs):
            key_rows, value_rows, length, new_key_rows, new_value_rows, new_rank = inputs
            scores = jnp.dot(query_rows, key_rows.T, preferred_element_type=jnp.float32) * score_scale
            usable = jnp.broadcast_to((positions < length).reshape(1, blocks, BLOCK), (row_total, blocks, BLOCK))
            scores = jnp.where(usable, scores.reshape(row_total, blocks, BLOCK), NEG_FILL)
            row_max = lax.optimization_barrier(jnp.max(scores, axis=2))
            weights = jnp.where(usable, jnp.exp(scores - row_max[..., None]), 0.0).astype(jnp.bfloat16)
            row_sum = lax.optimization_barrier(jnp.sum(weights.astype(jnp.float32), axis=2))
            summed = jnp.einsum('rnb,nbd->rnd', weights.astype(jnp.float32), value_rows.reshape(blocks, BLOCK, HD).astype(jnp.float32))
            for block_at in range(blocks):
                running = combine(running, (summed[:, block_at], row_max[:, block_at], row_sum[:, block_at]))
            usable_new = new_rank[None, :] <= rank_rows[:, None]
            running = combine(running, block_terms(query_rows, new_key_rows, new_value_rows, usable_new, score_scale))
            return (running, None)
        initial = (jnp.zeros((row_total, HD), jnp.float32), jnp.full((row_total,), NEG_FILL, jnp.float32), jnp.zeros((row_total,), jnp.float32))
        running, ignored = lax.scan(visit, initial, (shard_keys, shard_values, cache_len, span_keys, span_values, shard_rank))
        attended = (running[0] / running[2][:, None]).astype(jnp.bfloat16).reshape(SPAN, QPH * HD)
        pieces.append(attended)
    attended_all = jnp.concatenate(pieces, axis=1)
    return jnp.dot(attended_all, out_weight, preferred_element_type=jnp.float32).astype(jnp.bfloat16)
```

```python
import functools
import math

import jax
import jax.numpy as jnp
from jax import lax
from jax.experimental import pallas as pl
from jax.experimental.pallas import tpu as pltpu
from jax.sharding import PartitionSpec as P

NEG_FILL = -1e30
BF16 = jnp.bfloat16
F32 = jnp.float32
Z, YC, HEADS = 8, 4, 8
QPH, HD = 8, 128
TOK = 64
CACHE = 1024
GRAN = 128
CHUNK = 1024
SHARDS = 8
ROWS = TOK * QPH
VROWS = 144
WIDE = QPH * HD + 128
META = 2 * CACHE + 2 * TOK
BLOCK_ROWS = META + 16
KEYS = SHARDS * CACHE + CHUNK


def seq_permute(value, move):
    pairs = []
    for z in range(Z):
        for y in range(2):
            for c in range(2):
                to_z, to_y, to_c = move(z, y, c)
                pairs.append((z * 4 + y * 2 + c, (to_z % Z) * 4 + to_y * 2 + to_c))
    return lax.ppermute(value, "seq", pairs)


def attention_kernel(*refs):
    q_refs, kv_refs = refs[:4], refs[4:12]
    q_rank, k_rank = refs[12:14]
    outs = refs[14:18]
    q_all, k_all, v_all, new_k, new_v, m_all, acc = refs[18:]
    factor = F32(math.log2(math.e) / math.sqrt(HD))
    for b in range(4):
        for h in range(QPH):
            scaled = q_refs[b][:, h * HD : (h + 1) * HD].astype(F32) * factor
            high = scaled.astype(BF16)
            rows = pl.ds(b * ROWS + h * TOK, TOK)
            q_all[rows, 0:HD] = high
            q_all[rows, HD : 2 * HD] = (scaled - high.astype(F32)).astype(BF16)
    m_all[...] = jnp.full(m_all.shape, NEG_FILL, F32)
    acc[...] = jnp.zeros(acc.shape, F32)

    ones16 = (lax.broadcasted_iota(jnp.int32, (16, CACHE), 0) == 0).astype(F32)
    position = lax.broadcasted_iota(jnp.int32, (CACHE, HD), 0)
    lane_position = lax.broadcasted_iota(jnp.int32, (16, CACHE), 1)
    total = jnp.int32(0)
    for s in range(SHARDS):
        ref = kv_refs[s]
        meta = ref[META : META + 16, :].astype(F32).astype(jnp.int32)
        length = jnp.max(meta[0:8, :]) * 32 + jnp.max(meta[8:16, :])
        start = pl.multiple_of(total, GRAN)
        counted = position < length
        keys = ref[0:CACHE, :]
        keys = jnp.where(counted, keys, jnp.broadcast_to(keys[0:1, :], keys.shape))
        k_all[pl.ds(start, CACHE), 0:HD] = keys
        k_all[pl.ds(start, CACHE), HD : 2 * HD] = keys
        values = ref[CACHE : 2 * CACHE, :]
        values = jnp.where(counted, values, jnp.zeros_like(values))
        v_all[0:HD, pl.ds(start, CACHE)] = values.T
        flags = jnp.where(lane_position < length, ones16, 0.0).astype(BF16)
        v_all[HD:VROWS, pl.ds(start, CACHE)] = flags
        total = total + ((length + GRAN - 1) // GRAN) * GRAN
        rows = pl.ds(s * TOK, TOK)
        fresh = ref[2 * CACHE : 2 * CACHE + TOK, :]
        new_k[rows, 0:HD] = fresh
        new_k[rows, HD : 2 * HD] = fresh
        new_v[rows, :] = ref[2 * CACHE + TOK : META, :]
    filler = pl.ds(pl.multiple_of(total, GRAN), CHUNK)
    k_all[filler, :] = jnp.broadcast_to(k_all[0:1, :], (CHUNK, 2 * HD))
    v_all[:, filler] = jnp.zeros((VROWS, CHUNK), BF16)

    def scores(k, b):
        return lax.dot_general(
            k, q_all[b * ROWS : (b + 1) * ROWS, :], (((1,), (1,)), ((), ())),
            preferred_element_type=F32,
        )

    def weigh(s, b):
        cols = slice(b * ROWS, (b + 1) * ROWS)
        before = m_all[:, cols]
        top = jnp.maximum(before, jnp.max(s, axis=0, keepdims=True))
        m_all[:, cols] = top
        return jnp.exp2(s - top).astype(BF16), jnp.exp2(before - top)

    def add(p, scale, v, b):
        cols = slice(b * ROWS, (b + 1) * ROWS)
        acc[:, cols] = acc[:, cols] * scale + jnp.dot(v, p, preferred_element_type=F32)

    def step(k, v, mask=None):
        s = scores(k, 0)
        held = None
        for b in range(4):
            following = scores(k, b + 1) if b < 3 else None
            if mask is not None:
                s = jnp.where(mask(b), s, NEG_FILL)
            p, scale = weigh(s, b)
            if held is not None:
                add(*held)
            held = (p, scale, v, b)
            s = following
        add(*held)

    def cached(start, size):
        start = pl.multiple_of(start, GRAN)
        step(k_all[pl.ds(start, size), :], v_all[:, pl.ds(start, size)])

    whole = total // CHUNK
    rest = total - whole * CHUNK

    @pl.loop(0, whole)
    def _(i):
        cached(i * CHUNK, CHUNK)

    @pl.when(jnp.logical_and(rest > 0, rest <= CHUNK // 2))
    def _():
        cached(whole * CHUNK, CHUNK // 2)

    @pl.when(rest > CHUNK // 2)
    def _():
        cached(whole * CHUNK, CHUNK)

    new_vt = jnp.concatenate(
        [new_v[...].T, ones16[:, 0 : SHARDS * TOK].astype(BF16)], axis=0
    )
    step(
        new_k[...],
        new_vt,
        lambda b: k_rank[:, 0:1] <= q_rank[b : b + 1, :],
    )

    for b in range(4):
        stats = []
        for h in range(QPH):
            cols = slice(b * ROWS + h * TOK, b * ROWS + (h + 1) * TOK)
            held = acc[:, cols]
            weight = held[HD : HD + 1, :]
            outs[b][:, h * HD : (h + 1) * HD] = (held[0:HD, :] / weight).T.astype(BF16)
            stats.append(m_all[:, cols] + jnp.log2(weight))
        stats = jnp.concatenate(stats, axis=0)
        high = stats.astype(BF16).astype(F32)
        middle = (stats - high).astype(BF16).astype(F32)
        low = stats - high - middle
        stats = jnp.concatenate([high, middle, low, jnp.zeros((104, TOK), F32)], axis=0)
        outs[b][:, QPH * HD : WIDE] = stats.T.astype(BF16)


def attention(q_blocks, kv_blocks, q_rank, k_rank):
    return pl.pallas_call(
        attention_kernel,
        out_shape=[jax.ShapeDtypeStruct((TOK, WIDE), BF16)] * 4,
        scratch_shapes=[
            pltpu.VMEM((4 * ROWS, 2 * HD), BF16),
            pltpu.VMEM((KEYS, 2 * HD), BF16),
            pltpu.VMEM((VROWS, KEYS), BF16),
            pltpu.VMEM((SHARDS * TOK, 2 * HD), BF16),
            pltpu.VMEM((SHARDS * TOK, HD), BF16),
            pltpu.VMEM((1, 4 * ROWS), F32),
            pltpu.VMEM((VROWS, 4 * ROWS), F32),
        ],
        compiler_params=pltpu.CompilerParams(vmem_limit_bytes=56 * 2**20),
        name="attention",
    )(*q_blocks, *kv_blocks, q_rank, k_rank)


def merge_kernel(a_ref, b_ref, c_ref, d_ref, out_ref):
    parts = (a_ref, b_ref, c_ref, d_ref)
    stats = []
    for part in parts:
        lanes = part[:, QPH * HD : WIDE].astype(F32)
        stats.append(lanes[:, 0:8] + lanes[:, 8:16] + lanes[:, 16:24])
    top = functools.reduce(jnp.maximum, stats)
    shares = [jnp.exp2(s - top) for s in stats]
    whole = functools.reduce(jnp.add, shares)
    shares = [s / whole for s in shares]
    for h in range(QPH):
        cols = slice(h * HD, (h + 1) * HD)
        out_ref[:, cols] = functools.reduce(
            jnp.add,
            [p[:, cols].astype(F32) * s[:, h : h + 1] for p, s in zip(parts, shares)],
        ).astype(BF16)


def merge(parts):
    return pl.pallas_call(
        merge_kernel,
        out_shape=jax.ShapeDtypeStruct((TOK, QPH * HD), BF16),
        name="merge",
    )(*parts)


def body(queries, cache_keys, cache_values, new_keys, new_values, cache_len, span_rank, out_weight):
    seq = lax.axis_index("seq")
    z, yc = seq // 4, seq % 4
    y, c = yc // 2, yc % 2

    length = cache_len[0]
    meta = jnp.where(jnp.arange(16)[:, None] < 8, length // 32, length % 32)
    meta = jnp.broadcast_to(meta, (16, HD)).astype(BF16)
    own = jnp.concatenate([cache_keys[0], cache_values[0], new_keys, new_values, meta], axis=0)

    over_c = lambda v: seq_permute(v, lambda z, y, c: (z, y, 1 - c))
    kv_y = seq_permute(own, lambda z, y, c: (z, 1 - y, c))
    kv_z = seq_permute(own, lambda z, y, c: (z ^ 1, y, c))
    q_up = seq_permute(queries, lambda z, y, c: (z - 2, y, c))
    q_down = seq_permute(queries, lambda z, y, c: (z + 2, y, c))
    q_far = seq_permute(queries, lambda z, y, c: (z + 4, y, c))
    kv_yz = seq_permute(own, lambda z, y, c: (z ^ 1, 1 - y, c))
    kv = []
    for block in (own, kv_y, kv_z, kv_yz):
        kv += [block, over_c(block)]

    ranks = span_rank.reshape(Z, 2, 2, TOK)
    flip = lambda a, on, dim: jnp.where(on == 1, jnp.flip(a, dim), a)
    near = lax.dynamic_slice_in_dim(ranks, (z // 2) * 2, 2, 0)
    near = flip(flip(flip(near, z % 2, 0), y, 1), c, 2)
    k_rank = jnp.stack([near[0, 0], near[0, 1], near[1, 0], near[1, 1]]).reshape(SHARDS * TOK, 1)
    k_rank = jnp.broadcast_to(k_rank, (SHARDS * TOK, HD))
    by_z = lax.dynamic_index_in_dim(span_rank.reshape(Z, YC, TOK), yc, 1, False)
    steps = (z + jnp.array([4, 2, 6, 0])) % Z
    q_rank = jnp.tile(by_z[steps], (1, QPH))

    far, up, down, mine = attention((q_far, q_up, q_down, queries), kv, q_rank, k_rank)
    from_far = seq_permute(far, lambda z, y, c: (z + 4, y, c))
    from_down = seq_permute(up, lambda z, y, c: (z + 2, y, c))
    from_up = seq_permute(down, lambda z, y, c: (z - 2, y, c))
    attended = merge((from_far, from_down, from_up, mine))

    planes = [[z * 4 + i for i in range(YC)] for z in range(Z)]
    columns = [[z * 4 + i for z in range(Z)] for i in range(YC)]
    weights = lax.all_gather(out_weight, "seq", axis=0, axis_index_groups=columns)
    plane = lax.all_gather(attended, "seq", axis=0, tiled=True, axis_index_groups=planes)
    shares = jnp.einsum("tf,zfc->ztc", plane, weights, preferred_element_type=F32).astype(BF16)
    shares = lax.all_to_all(shares, "head", 0, 0, tiled=True)
    projected = jnp.sum(shares.astype(F32), axis=0).astype(BF16)
    swap = []
    for z in range(Z):
        for i in range(YC):
            for g in range(HEADS):
                swap.append(((z * YC + i) * HEADS + g, (g * YC + i) * HEADS + z))
    return lax.ppermute(projected, ("seq", "head"), swap)


def solution(mesh):
    return jax.shard_map(
        body,
        mesh=mesh,
        in_specs=(
            P("seq", "head"),
            P("head", "seq", None),
            P("head", "seq", None),
            P("seq", "head"),
            P("seq", "head"),
            P("seq"),
            P(),
            P("head", "seq"),
        ),
        out_specs=P("head", "seq"),
        check_vma=False,
    )
```

```python
import functools
import math

import jax
import jax.numpy as jnp
from jax import lax
from jax.experimental import pallas as pl
from jax.experimental.pallas import tpu as pltpu
from jax.sharding import PartitionSpec as P

NEG_FILL = -1e30
BF16 = jnp.bfloat16
F32 = jnp.float32
Z, YC = 8, 4
QPH, HD = 8, 128
TOK = 64
CACHE = 1024
GRAN = 128
CHUNK = 1024
PAIR = 2
ROWS = TOK * QPH
VROWS = 144
WIDE = QPH * HD + 128
KEY_ROWS = 2 * TOK + CACHE
VALUE_ROWS = CACHE + 16
KEYS = PAIR * CACHE + CHUNK


def seq_permute(value, move):
    pairs = []
    for z in range(Z):
        for y in range(2):
            for c in range(2):
                to_z, to_y, to_c = move(z, y, c)
                pairs.append((z * 4 + y * 2 + c, (to_z % Z) * 4 + to_y * 2 + to_c))
    return lax.ppermute(value, "seq", pairs)


def attention_kernel(first, last, key_at, value_at, *refs):
    refs = list(refs)
    take = lambda n: [refs.pop(0) for _ in range(n)]
    q_refs, key_refs, value_refs = take(4), take(PAIR), take(PAIR)
    if not first:
        m_in, acc_in = take(2)
    if last:
        new_refs = take(8)
        q_rank, k_rank = take(2)
        outs = take(4)
    m_all, acc = take(2)
    q_all, k_all, v_all = take(3)
    if last:
        new_k, new_v = take(2)
    factor = F32(math.log2(math.e) / math.sqrt(HD))
    for b in range(4):
        for h in range(QPH):
            scaled = q_refs[b][:, h * HD : (h + 1) * HD].astype(F32) * factor
            high = scaled.astype(BF16)
            rows = pl.ds(b * ROWS + h * TOK, TOK)
            q_all[rows, 0:HD] = high
            q_all[rows, HD : 2 * HD] = (scaled - high.astype(F32)).astype(BF16)
    if first:
        m_all[...] = jnp.full(m_all.shape, NEG_FILL, F32)
        acc[...] = jnp.zeros(acc.shape, F32)
    else:
        m_all[...] = m_in[...]
        acc[...] = acc_in[...]

    position = lax.broadcasted_iota(jnp.int32, (CACHE, HD), 0)
    lane_position = lax.broadcasted_iota(jnp.int32, (16, CACHE), 1)
    row16 = lax.broadcasted_iota(jnp.int32, (16, CACHE), 0)
    total = jnp.int32(0)
    for s in range(PAIR):
        meta = value_refs[s][value_at + CACHE : value_at + CACHE + 16, :].astype(F32).astype(jnp.int32)
        length = jnp.max(meta[0:8, :]) * 32 + jnp.max(meta[8:16, :])
        start = pl.multiple_of(total, GRAN)
        counted = position < length
        keys = key_refs[s][key_at : key_at + CACHE, :]
        keys = jnp.where(counted, keys, jnp.broadcast_to(keys[0:1, :], keys.shape))
        k_all[pl.ds(start, CACHE), 0:HD] = keys
        k_all[pl.ds(start, CACHE), HD : 2 * HD] = keys
        values = value_refs[s][value_at : value_at + CACHE, :]
        values = jnp.where(counted, values, jnp.zeros_like(values))
        v_all[0:HD, pl.ds(start, CACHE)] = values.T
        flags = jnp.logical_and(lane_position < length, row16 == 0)
        v_all[HD:VROWS, pl.ds(start, CACHE)] = jnp.where(flags, 1.0, 0.0).astype(BF16)
        total = total + ((length + GRAN - 1) // GRAN) * GRAN
    filler = pl.ds(pl.multiple_of(total, GRAN), 256)
    k_all[filler, :] = jnp.broadcast_to(k_all[0:1, :], (256, 2 * HD))
    v_all[:, filler] = jnp.zeros((VROWS, 256), BF16)

    def scores(k, b):
        return lax.dot_general(
            k, q_all[b * ROWS : (b + 1) * ROWS, :], (((1,), (1,)), ((), ())),
            preferred_element_type=F32,
        )

    def weigh(s, b):
        cols = slice(b * ROWS, (b + 1) * ROWS)
        before = m_all[:, cols]
        top = jnp.maximum(before, jnp.max(s, axis=0, keepdims=True))
        m_all[:, cols] = top
        return jnp.exp2(s - top).astype(BF16), jnp.exp2(before - top)

    def add(p, scale, v, b):
        cols = slice(b * ROWS, (b + 1) * ROWS)
        acc[:, cols] = acc[:, cols] * scale + jnp.dot(v, p, preferred_element_type=F32)

    def step(k, v, mask=None):
        s = scores(k, 0)
        held = None
        for b in range(4):
            following = scores(k, b + 1) if b < 3 else None
            if mask is not None:
                s = jnp.where(mask(b), s, NEG_FILL)
            p, scale = weigh(s, b)
            if held is not None:
                add(*held)
            held = (p, scale, v, b)
            s = following
        add(*held)

    def cached(start, size):
        start = pl.multiple_of(start, GRAN)
        step(k_all[pl.ds(start, size), :], v_all[:, pl.ds(start, size)])

    quarters = (total + 255) // 256
    whole = quarters // 4
    rest = quarters - whole * 4

    @pl.loop(0, whole)
    def _(i):
        cached(i * CHUNK, CHUNK)

    for size in (1, 2, 3):
        @pl.when(rest == size)
        def _():
            cached(whole * CHUNK, size * 256)

    if not last:
        return
    for s in range(8):
        rows = pl.ds(s * TOK, TOK)
        fresh = new_refs[s][0:TOK, :]
        new_k[rows, 0:HD] = fresh
        new_k[rows, HD : 2 * HD] = fresh
        new_v[rows, :] = new_refs[s][TOK : 2 * TOK, :]
    ones16 = jnp.where(row16[:, 0 : 8 * TOK] == 0, 1.0, 0.0).astype(BF16)
    step(
        new_k[...],
        jnp.concatenate([new_v[...].T, ones16], axis=0),
        lambda b: k_rank[:, 0:1] <= q_rank[b : b + 1, :],
    )
    for b in range(4):
        stats = []
        for h in range(QPH):
            cols = slice(b * ROWS + h * TOK, b * ROWS + (h + 1) * TOK)
            held = acc[:, cols]
            weight = held[HD : HD + 1, :]
            outs[b][:, h * HD : (h + 1) * HD] = (held[0:HD, :] / weight).T.astype(BF16)
            stats.append(m_all[:, cols] + jnp.log2(weight))
        stats = jnp.concatenate(stats, axis=0)
        high = stats.astype(BF16).astype(F32)
        middle = (stats - high).astype(BF16).astype(F32)
        low = stats - high - middle
        stats = jnp.concatenate([high, middle, low, jnp.zeros((104, TOK), F32)], axis=0)
        outs[b][:, QPH * HD : WIDE] = stats.T.astype(BF16)


def attention(q_blocks, keys, values, key_at, value_at, state=None, new=None, q_rank=None, k_rank=None):
    first, last = state is None, new is not None
    m_shape, acc_shape = (1, 4 * ROWS), (VROWS, 4 * ROWS)
    args = [*q_blocks, *keys, *values]
    whole = pl.BlockSpec(memory_space=pltpu.VMEM)
    specs = [whole] * len(args)
    if not first:
        args += state
        specs += [whole] * 2
    scratch = [
        pltpu.VMEM((4 * ROWS, 2 * HD), BF16),
        pltpu.VMEM((KEYS, 2 * HD), BF16),
        pltpu.VMEM((VROWS, KEYS), BF16),
    ]
    if last:
        args += [*new, q_rank, k_rank]
        specs += [pl.BlockSpec((2 * TOK, HD), lambda i: (0, 0))] * 8 + [whole] * 2
        out_shape = [jax.ShapeDtypeStruct((TOK, WIDE), BF16)] * 4
        scratch = [
            pltpu.VMEM(m_shape, F32),
            pltpu.VMEM(acc_shape, F32),
            *scratch,
            pltpu.VMEM((8 * TOK, 2 * HD), BF16),
            pltpu.VMEM((8 * TOK, HD), BF16),
        ]
    else:
        out_shape = [jax.ShapeDtypeStruct(m_shape, F32), jax.ShapeDtypeStruct(acc_shape, F32)]
    return pl.pallas_call(
        functools.partial(attention_kernel, first, last, key_at, value_at),
        grid=(1,),
        out_shape=out_shape,
        in_specs=specs,
        out_specs=[whole] * len(out_shape),
        scratch_shapes=scratch,
        compiler_params=pltpu.CompilerParams(vmem_limit_bytes=56 * 2**20),
        name="attention",
    )(*args)


def merge_kernel(a_ref, b_ref, c_ref, d_ref, out_ref):
    parts = (a_ref, b_ref, c_ref, d_ref)
    stats = []
    for part in parts:
        lanes = part[:, QPH * HD : WIDE].astype(F32)
        stats.append(lanes[:, 0:8] + lanes[:, 8:16] + lanes[:, 16:24])
    top = functools.reduce(jnp.maximum, stats)
    shares = [jnp.exp2(s - top) for s in stats]
    whole = functools.reduce(jnp.add, shares)
    shares = [s / whole for s in shares]
    for h in range(QPH):
        cols = slice(h * HD, (h + 1) * HD)
        out_ref[:, cols] = functools.reduce(
            jnp.add,
            [p[:, cols].astype(F32) * s[:, h : h + 1] for p, s in zip(parts, shares)],
        ).astype(BF16)


def merge(parts):
    return pl.pallas_call(
        merge_kernel,
        out_shape=jax.ShapeDtypeStruct((TOK, QPH * HD), BF16),
        name="merge",
    )(*parts)


def product_kernel(z_ref, *refs):
    blocks, weights, out_ref, every = refs[:8], refs[8:12], refs[12], refs[13]
    z = z_ref[0]
    for k in range(Z):
        every[(z + k) % Z] = blocks[k][...]
    rows = every[...].reshape(Z * TOK, QPH * HD)
    for r in range(YC):
        part = jnp.dot(rows, weights[r][...], preferred_element_type=F32)
        out_ref[:, :, r * 256 : (r + 1) * 256] = part.astype(BF16).reshape(Z, TOK, 256)


def product(z, blocks, weights):
    whole = pl.BlockSpec(memory_space=pltpu.VMEM)
    return pl.pallas_call(
        product_kernel,
        out_shape=jax.ShapeDtypeStruct((Z, TOK, YC * 256), BF16),
        in_specs=[pl.BlockSpec(memory_space=pltpu.SMEM)] + [whole] * 12,
        out_specs=whole,
        scratch_shapes=[pltpu.VMEM((Z, TOK, QPH * HD), BF16)],
        compiler_params=pltpu.CompilerParams(vmem_limit_bytes=56 * 2**20),
        name="product",
    )(z.reshape(1), *blocks, *weights)


def body(queries, cache_keys, cache_values, new_keys, new_values, cache_len, span_rank, out_weight):
    seq = lax.axis_index("seq")
    z, yc = seq // 4, seq % 4
    y, c = yc // 2, yc % 2

    length = cache_len[0]
    meta = jnp.where(jnp.arange(16)[:, None] < 8, length // 32, length % 32)
    meta = jnp.broadcast_to(meta, (16, HD)).astype(BF16)
    own = jnp.concatenate([new_keys, new_values, cache_keys[0], cache_values[0], meta], axis=0)

    over_c = lambda v: seq_permute(v, lambda z, y, c: (z, y, 1 - c))
    over_y = lambda v: seq_permute(v, lambda z, y, c: (z, 1 - y, c))
    over_z = lambda v: seq_permute(v, lambda z, y, c: (z ^ 1, y, c))
    shift = lambda v, n: seq_permute(v, lambda z, y, c: (z + n, y, c))
    kv_y, kv_z = over_y(own), over_z(own)
    q_blocks = (shift(queries, 4), shift(queries, -2), shift(queries, 2), queries)

    ranks = span_rank.reshape(Z, 2, 2, TOK)
    flip = lambda a, on, dim: jnp.where(on == 1, jnp.flip(a, dim), a)
    near = lax.dynamic_slice_in_dim(ranks, (z // 2) * 2, 2, 0)
    near = flip(flip(flip(near, z % 2, 0), y, 1), c, 2)
    k_rank = jnp.stack([near[0, 0], near[0, 1], near[1, 0], near[1, 1]]).reshape(8 * TOK, 1)
    k_rank = jnp.broadcast_to(k_rank, (8 * TOK, HD))
    by_z = lax.dynamic_index_in_dim(span_rank.reshape(Z, YC, TOK), yc, 1, False)
    steps = (z + jnp.array([4, 2, 6, 0])) % Z
    q_rank = jnp.tile(by_z[steps], (1, QPH))

    near_pair = (own, over_c(own))
    state = attention(q_blocks, near_pair, near_pair, 2 * TOK, KEY_ROWS)
    kv_y, kv_z, *state = lax.optimization_barrier((kv_y, kv_z, *state))
    far_keys, far_values = over_y(kv_z[:KEY_ROWS]), over_z(kv_y[KEY_ROWS:])
    y_pair, z_pair = (kv_y, over_c(kv_y)), (kv_z, over_c(kv_z))
    state = attention(q_blocks, y_pair, y_pair, 2 * TOK, KEY_ROWS, state)
    state = attention(q_blocks, z_pair, z_pair, 2 * TOK, KEY_ROWS, state)
    far_keys, far_values, *state = lax.optimization_barrier((far_keys, far_values, *state))
    keys, values = (far_keys, over_c(far_keys)), (far_values, over_c(far_values))
    new = (*near_pair, *y_pair, *z_pair, *keys)
    far, up, down, mine = attention(q_blocks, keys, values, 2 * TOK, 0, state, new, q_rank, k_rank)
    attended = merge((shift(far, 4), shift(up, 2), shift(down, -2), mine))

    weight = lax.optimization_barrier((out_weight, far_keys, far_values))[0]
    weight_y = over_y(weight)
    weights = [out_weight, over_c(weight), weight_y, over_c(weight_y)]

    blocks = [None] * Z
    blocks[0] = attended
    for k in (1, 2, 3):
        blocks[k] = shift(blocks[k - 1], -1)
        blocks[Z - k] = shift(blocks[(Z - k + 1) % Z], 1)
    blocks[4] = shift(blocks[3], -1)
    shares = product(z, blocks, weights)
    shares = lax.all_to_all(shares, "head", 0, 0, tiled=True)
    mine = jnp.sum(shares.astype(F32), axis=0).astype(BF16).reshape(TOK, YC, 256)
    from_c = over_c(mine[:, 1])
    from_y = over_y(mine[:, 2:])
    parts = [[mine[:, 0], from_c], [from_y[:, 0], over_c(from_y[:, 1])]]
    parts = jnp.stack([jnp.stack(p) for p in parts])
    return flip(flip(parts, y, 0), c, 1).reshape(YC * TOK, 256)


def solution(mesh):
    return jax.shard_map(
        body,
        mesh=mesh,
        in_specs=(
            P("seq", "head"),
            P("head", "seq", None),
            P("head", "seq", None),
            P("seq", "head"),
            P("seq", "head"),
            P("seq"),
            P(),
            P("head", "seq"),
        ),
        out_specs=P("head", "seq"),
        check_vma=False,
    )
```

```python
import functools
import math

import jax
import jax.numpy as jnp
from jax import lax
from jax.experimental import pallas as pl
from jax.experimental.pallas import tpu as pltpu
from jax.sharding import PartitionSpec as P

NEG_FILL = -1e30
BF16 = jnp.bfloat16
F32 = jnp.float32
Z, YC = 8, 4
QPH, HD = 8, 128
TOK = 64
CACHE = 1024
GRAN = 128
CHUNK = 512
BLOCKS = 4
ROWS = TOK * QPH
TILE = 2 * ROWS
VROWS = 144
WIDE = QPH * HD + 128
KEY_AT = 2 * TOK
VALUE_AT = KEY_AT + CACHE
META_AT = VALUE_AT + CACHE
BLOCK_ROWS = META_AT + 16
PLANES = [[z * YC + i for i in range(YC)] for z in range(Z)]


def seq_permute(value, move):
    pairs = []
    for z in range(Z):
        for y in range(2):
            for c in range(2):
                to_z, to_y, to_c = move(z, y, c)
                pairs.append((z * 4 + y * 2 + c, (to_z % Z) * 4 + to_y * 2 + to_c))
    return lax.ppermute(value, "seq", pairs)


def pack_kernel(length_ref, k_ref, v_ref, nk_ref, nv_ref, out_ref):
    length = length_ref[0]
    out_ref[0:TOK, :] = nk_ref[...]
    out_ref[TOK:KEY_AT, :] = nv_ref[...]
    out_ref[KEY_AT:VALUE_AT, :] = k_ref[0]
    out_ref[VALUE_AT:META_AT, :] = v_ref[0]
    row = lax.broadcasted_iota(jnp.int32, (16, HD), 0)
    meta = jnp.where(row < 8, length // 32, length % 32)
    out_ref[META_AT:BLOCK_ROWS, :] = meta.astype(F32).astype(BF16)


def pack(length, keys, values, new_keys, new_values):
    whole = pl.BlockSpec(memory_space=pltpu.VMEM)
    return pl.pallas_call(
        pack_kernel,
        out_shape=jax.ShapeDtypeStruct((BLOCK_ROWS, HD), BF16),
        in_specs=[pl.BlockSpec(memory_space=pltpu.SMEM)] + [whole] * 4,
        out_specs=whole,
        name="pack",
    )(length, keys, values, new_keys, new_values)


def attention_kernel(shards, first, last, *refs):
    refs = list(refs)
    take = lambda n: [refs.pop(0) for _ in range(n)]
    q_refs, shard_refs = take(BLOCKS), take(shards)
    if not first:
        m_in, acc_in = take(2)
    if last:
        new_refs = take(8)
        q_rank, k_rank = take(2)
        out_refs = take(BLOCKS)
    m_all, acc = take(2)
    q_all, k_all, v_all, s0, s1, p0, p1, scale0, scale1 = take(9)
    if last:
        new_k, new_v = take(2)
    factor = F32(math.log2(math.e) / math.sqrt(HD))
    for b in range(BLOCKS):
        for h in range(QPH):
            scaled = q_refs[b][:, h * HD : (h + 1) * HD].astype(F32) * factor
            high = scaled.astype(BF16)
            rows = pl.ds(b * ROWS + h * TOK, TOK)
            q_all[rows, 0:HD] = high
            q_all[rows, HD : 2 * HD] = (scaled - high.astype(F32)).astype(BF16)
    if first:
        m_all[...] = jnp.full(m_all.shape, NEG_FILL, F32)
        acc[...] = jnp.zeros(acc.shape, F32)
    else:
        m_all[...] = m_in[...]
        acc[...] = acc_in[...]

    position = lax.broadcasted_iota(jnp.int32, (CACHE, HD), 0)
    lane_position = lax.broadcasted_iota(jnp.int32, (16, CACHE), 1)
    row16 = lax.broadcasted_iota(jnp.int32, (16, CACHE), 0)
    total = jnp.int32(0)
    for ref in shard_refs:
        meta = ref[META_AT:BLOCK_ROWS, :].astype(F32).astype(jnp.int32)
        length = jnp.max(meta[0:8, :]) * 32 + jnp.max(meta[8:16, :])
        start = pl.multiple_of(total, GRAN)
        counted = position < length
        keys = ref[KEY_AT:VALUE_AT, :]
        keys = jnp.where(counted, keys, jnp.broadcast_to(keys[0:1, :], keys.shape))
        k_all[pl.ds(start, CACHE), 0:HD] = keys
        k_all[pl.ds(start, CACHE), HD : 2 * HD] = keys
        values = ref[VALUE_AT:META_AT, :]
        values = jnp.where(counted, values, jnp.zeros_like(values))
        v_all[0:HD, pl.ds(start, CACHE)] = values.T
        flags = jnp.logical_and(lane_position < length, row16 == 0)
        v_all[HD:VROWS, pl.ds(start, CACHE)] = jnp.where(flags, 1.0, 0.0).astype(BF16)
        total = total + ((length + GRAN - 1) // GRAN) * GRAN
    filler = pl.ds(pl.multiple_of(total, GRAN), CHUNK)
    k_all[filler, :] = jnp.broadcast_to(k_all[0:1, :], (CHUNK, 2 * HD))
    v_all[:, filler] = jnp.zeros((VROWS, CHUNK), BF16)

    left, right = slice(0, TILE), slice(TILE, 2 * TILE)

    def scores(s, k, rows):
        s[...] = lax.dot_general(
            k, q_all[rows, :], (((1,), (1,)), ((), ())), preferred_element_type=F32
        )

    def weigh(s, p, scale, rows):
        before = m_all[:, rows]
        top = jnp.maximum(before, jnp.max(s, axis=0, keepdims=True))
        m_all[:, rows] = top
        p[...] = jnp.exp2(s - top).astype(BF16)
        scale[...] = jnp.exp2(before - top)

    def add(p, scale, v, rows):
        acc[:, rows] = acc[:, rows] * scale[...] + jnp.dot(
            v, p[...], preferred_element_type=F32
        )

    def chunk(i):
        return pl.ds(pl.multiple_of(i * CHUNK, CHUNK), CHUNK)

    count = (total + CHUNK - 1) // CHUNK
    p1[...] = jnp.zeros(p1.shape, BF16)
    scale1[...] = jnp.ones(scale1.shape, F32)
    scores(s0, k_all[0:CHUNK, :], left)

    @pl.loop(0, count)
    def _(i):
        before, here = chunk(jnp.maximum(i - 1, 0)), chunk(i)
        after = chunk(jnp.minimum(i + 1, count - 1))
        scores(s1, k_all[here, :], right)
        weigh(s0[...], p0, scale0, left)
        add(p1, scale1, v_all[:, before], right)
        scores(s0, k_all[after, :], left)
        weigh(s1[...], p1, scale1, right)
        add(p0, scale0, v_all[:, here], left)

    add(p1, scale1, v_all[:, chunk(count - 1)], right)
    if not last:
        return
    for s in range(8):
        rows = pl.ds(s * TOK, TOK)
        fresh = new_refs[s][0:TOK, :]
        new_k[rows, 0:HD] = fresh
        new_k[rows, HD : 2 * HD] = fresh
        new_v[rows, :] = new_refs[s][TOK : 2 * TOK, :]
    ones16 = jnp.where(row16[:, 0:CHUNK] == 0, 1.0, 0.0).astype(BF16)
    values = jnp.concatenate([new_v[...].T, ones16], axis=0)
    scores(s0, new_k[...], left)
    scores(s1, new_k[...], right)
    ranks = k_rank[:, 0:1]
    weigh(jnp.where(ranks <= q_rank[:, left], s0[...], NEG_FILL), p0, scale0, left)
    add(p0, scale0, values, left)
    weigh(jnp.where(ranks <= q_rank[:, right], s1[...], NEG_FILL), p1, scale1, right)
    add(p1, scale1, values, right)
    for b in range(BLOCKS):
        stats = []
        for h in range(QPH):
            cols = slice(b * ROWS + h * TOK, b * ROWS + (h + 1) * TOK)
            held = acc[:, cols]
            weight = held[HD : HD + 1, :]
            out_refs[b][:, h * HD : (h + 1) * HD] = (held[0:HD, :] / weight).T.astype(BF16)
            stats.append(m_all[:, cols] + jnp.log2(weight))
        stats = jnp.concatenate(stats, axis=0)
        high = stats.astype(BF16).astype(F32)
        middle = (stats - high).astype(BF16).astype(F32)
        low = stats - high - middle
        stats = jnp.concatenate([high, middle, low, jnp.zeros((104, TOK), F32)], axis=0)
        out_refs[b][:, QPH * HD : WIDE] = stats.T.astype(BF16)


def attention(q_blocks, shards, state=None, new=None, q_rank=None, k_rank=None):
    first, last = state is None, new is not None
    m_shape, acc_shape = (1, BLOCKS * ROWS), (VROWS, BLOCKS * ROWS)
    args = [*q_blocks, *shards]
    whole = pl.BlockSpec(memory_space=pltpu.VMEM)
    specs = [whole] * len(args)
    if not first:
        args += state
        specs += [whole] * 2
    keys = len(shards) * CACHE + CHUNK
    scratch = [
        pltpu.VMEM((BLOCKS * ROWS, 2 * HD), BF16),
        pltpu.VMEM((keys, 2 * HD), BF16),
        pltpu.VMEM((VROWS, keys), BF16),
        pltpu.VMEM((CHUNK, TILE), F32),
        pltpu.VMEM((CHUNK, TILE), F32),
        pltpu.VMEM((CHUNK, TILE), BF16),
        pltpu.VMEM((CHUNK, TILE), BF16),
        pltpu.VMEM((1, TILE), F32),
        pltpu.VMEM((1, TILE), F32),
    ]
    if last:
        args += [*new, q_rank, k_rank]
        specs += [pl.BlockSpec((2 * TOK, HD), lambda i: (0, 0))] * 8 + [whole] * 2
        out_shape = [jax.ShapeDtypeStruct((TOK, WIDE), BF16)] * BLOCKS
        out_specs = [whole] * BLOCKS
        scratch = [
            pltpu.VMEM(m_shape, F32),
            pltpu.VMEM(acc_shape, F32),
            *scratch,
            pltpu.VMEM((8 * TOK, 2 * HD), BF16),
            pltpu.VMEM((8 * TOK, HD), BF16),
        ]
    else:
        out_shape = [jax.ShapeDtypeStruct(m_shape, F32), jax.ShapeDtypeStruct(acc_shape, F32)]
        out_specs = [whole] * 2
    return pl.pallas_call(
        functools.partial(attention_kernel, len(shards), first, last),
        grid=(1,),
        out_shape=out_shape,
        in_specs=specs,
        out_specs=out_specs,
        scratch_shapes=scratch,
        compiler_params=pltpu.CompilerParams(vmem_limit_bytes=56 * 2**20),
        name="attention",
    )(*args)


def merge_kernel(*refs):
    parts, out_ref = refs[:BLOCKS], refs[BLOCKS]
    stats = []
    for b in range(BLOCKS):
        lanes = parts[b][:, QPH * HD : WIDE].astype(F32)
        stats.append(lanes[:, 0:8] + lanes[:, 8:16] + lanes[:, 16:24])
    top = functools.reduce(jnp.maximum, stats)
    shares = [jnp.exp2(s - top) for s in stats]
    whole = functools.reduce(jnp.add, shares)
    shares = [s / whole for s in shares]
    for h in range(QPH):
        cols = slice(h * HD, (h + 1) * HD)
        out_ref[:, cols] = functools.reduce(
            jnp.add,
            [parts[b][:, cols].astype(F32) * shares[b][:, h : h + 1] for b in range(BLOCKS)],
        ).astype(BF16)


def merge(parts):
    return pl.pallas_call(
        merge_kernel,
        out_shape=jax.ShapeDtypeStruct((TOK, QPH * HD), BF16),
        name="merge",
    )(*parts)


def product_kernel(place_ref, *refs):
    blocks, weights, out_ref, every = refs[:8], refs[8:12], refs[12], refs[13]
    z, yc = place_ref[0], place_ref[1]
    for k in range(Z):
        every[(z + k) % Z] = blocks[k][...]
    rows = every[...].reshape(Z * TOK, QPH * HD)
    for r in range(YC):
        part = jnp.dot(rows, weights[r][...], preferred_element_type=F32)
        out_ref[:, yc ^ r] = part.astype(BF16).reshape(Z, TOK, 256)


def product(place, blocks, weights):
    whole = pl.BlockSpec(memory_space=pltpu.VMEM)
    return pl.pallas_call(
        product_kernel,
        out_shape=jax.ShapeDtypeStruct((Z, YC, TOK, 256), BF16),
        in_specs=[pl.BlockSpec(memory_space=pltpu.SMEM)] + [whole] * 12,
        out_specs=whole,
        scratch_shapes=[pltpu.VMEM((Z, TOK, QPH * HD), BF16)],
        compiler_params=pltpu.CompilerParams(vmem_limit_bytes=56 * 2**20),
        name="product",
    )(place, *blocks, *weights)


def body(queries, cache_keys, cache_values, new_keys, new_values, cache_len, span_rank, out_weight):
    seq = lax.axis_index("seq")
    z, yc = seq // YC, seq % YC
    y, c = yc // 2, yc % 2

    own = pack(cache_len, cache_keys, cache_values, new_keys, new_values)
    over_c = lambda v: seq_permute(v, lambda z, y, c: (z, y, 1 - c))
    over_y = lambda v: seq_permute(v, lambda z, y, c: (z, 1 - y, c))
    over_z = lambda v: seq_permute(v, lambda z, y, c: (z ^ 1, y, c))
    shift = lambda v, n: seq_permute(v, lambda z, y, c: (z + n, y, c))

    kv_y = over_y(own)
    own_pair = (own, over_c(own))
    q_blocks = (shift(queries, 4), shift(queries, -2), shift(queries, 2), queries)
    sent, *q_blocks = lax.optimization_barrier((own, *q_blocks))
    kv_z = over_z(sent)
    kv_yz = over_z(kv_y)

    ranks = span_rank.reshape(Z, 2, 2, TOK)
    flip = lambda a, on, dim: jnp.where(on == 1, jnp.flip(a, dim), a)
    near = lax.dynamic_slice_in_dim(ranks, (z // 2) * 2, 2, 0)
    near = flip(flip(flip(near, z % 2, 0), y, 1), c, 2)
    k_rank = jnp.stack([near[0, 0], near[0, 1], near[1, 0], near[1, 1]]).reshape(8 * TOK, 1)
    k_rank = jnp.broadcast_to(k_rank, (8 * TOK, HD))
    by_z = lax.dynamic_index_in_dim(span_rank.reshape(Z, YC, TOK), yc, 1, False)
    steps = (z + jnp.array([4, 2, 6, 0])) % Z
    q_rank = jnp.tile(by_z[steps], (1, QPH)).reshape(1, BLOCKS * ROWS)

    y_pair = (kv_y, over_c(kv_y))
    state = attention(q_blocks, (*own_pair, *y_pair))
    kv_z, kv_yz, *state = lax.optimization_barrier((kv_z, kv_yz, *state))
    z_pair = (kv_z, over_c(kv_z))
    yz_pair = (kv_yz, over_c(kv_yz))
    state = attention(q_blocks, z_pair, state)
    new = (*own_pair, *y_pair, *z_pair, *yz_pair)
    far, up, down, mine = attention(q_blocks, yz_pair, state, new, q_rank, k_rank)
    attended = merge((shift(far, 4), shift(up, 2), shift(down, -2), mine))

    weight = lax.optimization_barrier((out_weight, kv_yz))[0]
    weight_y = over_y(weight)
    weights = [out_weight, over_c(weight), weight_y, over_c(weight_y)]

    blocks = [None] * Z
    blocks[0] = attended
    for k in (1, 2, 3):
        blocks[k] = shift(blocks[k - 1], -1)
        blocks[Z - k] = shift(blocks[(Z - k + 1) % Z], 1)
    blocks[4] = shift(blocks[3], -1)
    shares = product(jnp.stack([z, yc]), blocks, weights)
    shares = lax.all_to_all(shares, "head", 0, 0, tiled=True)
    projected = jnp.sum(shares.astype(F32), axis=0).astype(BF16)
    projected = lax.all_to_all(projected, "seq", 0, 0, axis_index_groups=PLANES, tiled=True)
    return projected.reshape(YC * TOK, 256)


def solution(mesh):
    return jax.shard_map(
        body,
        mesh=mesh,
        in_specs=(
            P("seq", "head"),
            P("head", "seq", None),
            P("head", "seq", None),
            P("seq", "head"),
            P("seq", "head"),
            P("seq"),
            P(),
            P("head", "seq"),
        ),
        out_specs=P("head", "seq"),
        check_vma=False,
    )
```

```python
import functools
import math

import jax
import jax.numpy as jnp
from jax import lax
from jax.experimental import pallas as pl
from jax.experimental.pallas import tpu as pltpu
from jax.sharding import PartitionSpec as P

NEG_FILL = -1e30
BF16 = jnp.bfloat16
F32 = jnp.float32
Z, YC = 8, 4
QPH, HD = 8, 128
TOK = 64
CACHE = 1024
GRAN = 128
CHUNK = 512
BLOCKS = 4
ROWS = TOK * QPH
TILE = 2 * ROWS
VROWS = 144
WIDE = QPH * HD + 128
KEY_AT = 2 * TOK
VALUE_AT = KEY_AT + CACHE
META_AT = VALUE_AT + CACHE
BLOCK_ROWS = META_AT + 16
PLANES = [[z * YC + i for i in range(YC)] for z in range(Z)]


def seq_permute(value, move):
    pairs = []
    for z in range(Z):
        for y in range(2):
            for c in range(2):
                to_z, to_y, to_c = move(z, y, c)
                pairs.append((z * 4 + y * 2 + c, (to_z % Z) * 4 + to_y * 2 + to_c))
    return lax.ppermute(value, "seq", pairs)


def pack_kernel(length_ref, k_ref, v_ref, nk_ref, nv_ref, out_ref):
    length = length_ref[0]
    out_ref[0:TOK, :] = nk_ref[...]
    out_ref[TOK:KEY_AT, :] = nv_ref[...]
    out_ref[KEY_AT:VALUE_AT, :] = k_ref[0]
    out_ref[VALUE_AT:META_AT, :] = v_ref[0]
    row = lax.broadcasted_iota(jnp.int32, (16, HD), 0)
    meta = jnp.where(row < 8, length // 32, length % 32)
    out_ref[META_AT:BLOCK_ROWS, :] = meta.astype(F32).astype(BF16)


def pack(length, keys, values, new_keys, new_values):
    whole = pl.BlockSpec(memory_space=pltpu.VMEM)
    return pl.pallas_call(
        pack_kernel,
        out_shape=jax.ShapeDtypeStruct((BLOCK_ROWS, HD), BF16),
        in_specs=[pl.BlockSpec(memory_space=pltpu.SMEM)] + [whole] * 4,
        out_specs=whole,
        name="pack",
    )(length, keys, values, new_keys, new_values)


def attention_kernel(shards, first, last, *refs):
    refs = list(refs)
    take = lambda n: [refs.pop(0) for _ in range(n)]
    q_refs, shard_refs = take(BLOCKS), take(shards)
    if not first:
        m_in, acc_in = take(2)
    if last:
        new_refs = take(8)
        q_rank, k_rank = take(2)
        out_refs = take(BLOCKS)
    m_all, acc = take(2)
    q_all, k_all, v_all, s0, s1, p0, p1, scale0, scale1 = take(9)
    if last:
        new_k, new_v = take(2)
    factor = F32(math.log2(math.e) / math.sqrt(HD))
    for b in range(BLOCKS):
        for h in range(QPH):
            scaled = q_refs[b][:, h * HD : (h + 1) * HD].astype(F32) * factor
            high = scaled.astype(BF16)
            rows = pl.ds(b * ROWS + h * TOK, TOK)
            q_all[rows, 0:HD] = high
            q_all[rows, HD : 2 * HD] = (scaled - high.astype(F32)).astype(BF16)
    if first:
        m_all[...] = jnp.full(m_all.shape, NEG_FILL, F32)
        acc[...] = jnp.zeros(acc.shape, F32)
    else:
        m_all[...] = m_in[...]
        acc[...] = acc_in[...]

    position = lax.broadcasted_iota(jnp.int32, (CACHE, HD), 0)
    lane_position = lax.broadcasted_iota(jnp.int32, (16, CACHE), 1)
    row16 = lax.broadcasted_iota(jnp.int32, (16, CACHE), 0)
    lengths = []
    for ref in shard_refs:
        meta = ref[META_AT:BLOCK_ROWS, :].astype(F32)
        lengths.append(jnp.max(meta[0:8, :] * 32.0 + meta[8:16, :]).astype(jnp.int32))
    total = jnp.int32(0)
    for ref, length in zip(shard_refs, lengths):
        start = pl.multiple_of(total, GRAN)
        counted = position < length
        keys = ref[KEY_AT:VALUE_AT, :]
        keys = jnp.where(counted, keys, jnp.broadcast_to(keys[0:1, :], keys.shape))
        k_all[pl.ds(start, CACHE), 0:HD] = keys
        k_all[pl.ds(start, CACHE), HD : 2 * HD] = keys
        values = ref[VALUE_AT:META_AT, :]
        values = jnp.where(counted, values, jnp.zeros_like(values))
        v_all[0:HD, pl.ds(start, CACHE)] = values.T
        flags = jnp.logical_and(lane_position < length, row16 == 0)
        v_all[HD:VROWS, pl.ds(start, CACHE)] = jnp.where(flags, 1.0, 0.0).astype(BF16)
        total = total + ((length + GRAN - 1) // GRAN) * GRAN
    filler = pl.ds(pl.multiple_of(total, GRAN), CHUNK)
    k_all[filler, :] = jnp.broadcast_to(k_all[0:1, :], (CHUNK, 2 * HD))
    v_all[:, filler] = jnp.zeros((VROWS, CHUNK), BF16)

    left, right = slice(0, TILE), slice(TILE, 2 * TILE)

    def scores(s, k, rows):
        s[...] = lax.dot_general(
            k, q_all[rows, :], (((1,), (1,)), ((), ())), preferred_element_type=F32
        )

    def weigh(s, p, scale, rows):
        before = m_all[:, rows]
        top = jnp.maximum(before, jnp.max(s, axis=0, keepdims=True))
        m_all[:, rows] = top
        p[...] = jnp.exp2(s - top).astype(BF16)
        scale[...] = jnp.exp2(before - top)

    def add(p, scale, v, rows):
        acc[:, rows] = acc[:, rows] * scale[...] + jnp.dot(
            v, p[...], preferred_element_type=F32
        )

    def chunk(i):
        return pl.ds(pl.multiple_of(i * CHUNK, CHUNK), CHUNK)

    count = (total + CHUNK - 1) // CHUNK
    p1[...] = jnp.zeros(p1.shape, BF16)
    scale1[...] = jnp.ones(scale1.shape, F32)
    scores(s0, k_all[0:CHUNK, :], left)

    @pl.loop(0, count)
    def _(i):
        before, here = chunk(jnp.maximum(i - 1, 0)), chunk(i)
        after = chunk(jnp.minimum(i + 1, count - 1))
        scores(s1, k_all[here, :], right)
        weigh(s0[...], p0, scale0, left)
        add(p1, scale1, v_all[:, before], right)
        scores(s0, k_all[after, :], left)
        weigh(s1[...], p1, scale1, right)
        add(p0, scale0, v_all[:, here], left)

    add(p1, scale1, v_all[:, chunk(count - 1)], right)
    if not last:
        return
    for s in range(8):
        rows = pl.ds(s * TOK, TOK)
        fresh = new_refs[s][0:TOK, :]
        new_k[rows, 0:HD] = fresh
        new_k[rows, HD : 2 * HD] = fresh
        new_v[rows, :] = new_refs[s][TOK : 2 * TOK, :]
    ones16 = jnp.where(row16[:, 0:CHUNK] == 0, 1.0, 0.0).astype(BF16)
    values = jnp.concatenate([new_v[...].T, ones16], axis=0)
    scores(s0, new_k[...], left)
    scores(s1, new_k[...], right)
    ranks = k_rank[:, 0:1]
    weigh(jnp.where(ranks <= q_rank[:, left], s0[...], NEG_FILL), p0, scale0, left)
    add(p0, scale0, values, left)
    weigh(jnp.where(ranks <= q_rank[:, right], s1[...], NEG_FILL), p1, scale1, right)
    add(p1, scale1, values, right)
    for b in range(BLOCKS):
        stats = []
        for h in range(QPH):
            cols = slice(b * ROWS + h * TOK, b * ROWS + (h + 1) * TOK)
            held = acc[:, cols]
            weight = held[HD : HD + 1, :]
            out_refs[b][:, h * HD : (h + 1) * HD] = (held[0:HD, :] / weight).T.astype(BF16)
            stats.append(m_all[:, cols] + jnp.log2(weight))
        stats = jnp.concatenate(stats, axis=0)
        high = stats.astype(BF16).astype(F32)
        middle = (stats - high).astype(BF16).astype(F32)
        low = stats - high - middle
        stats = jnp.concatenate([high, middle, low, jnp.zeros((104, TOK), F32)], axis=0)
        out_refs[b][:, QPH * HD : WIDE] = stats.T.astype(BF16)


def attention(q_blocks, shards, state=None, new=None, q_rank=None, k_rank=None):
    first, last = state is None, new is not None
    m_shape, acc_shape = (1, BLOCKS * ROWS), (VROWS, BLOCKS * ROWS)
    args = [*q_blocks, *shards]
    whole = pl.BlockSpec(memory_space=pltpu.VMEM)
    specs = [whole] * len(args)
    if not first:
        args += state
        specs += [whole] * 2
    keys = len(shards) * CACHE + CHUNK
    scratch = [
        pltpu.VMEM((BLOCKS * ROWS, 2 * HD), BF16),
        pltpu.VMEM((keys, 2 * HD), BF16),
        pltpu.VMEM((VROWS, keys), BF16),
        pltpu.VMEM((CHUNK, TILE), F32),
        pltpu.VMEM((CHUNK, TILE), F32),
        pltpu.VMEM((CHUNK, TILE), BF16),
        pltpu.VMEM((CHUNK, TILE), BF16),
        pltpu.VMEM((1, TILE), F32),
        pltpu.VMEM((1, TILE), F32),
    ]
    if last:
        args += [*new, q_rank, k_rank]
        specs += [pl.BlockSpec((2 * TOK, HD), lambda i: (0, 0))] * 8 + [whole] * 2
        out_shape = [jax.ShapeDtypeStruct((TOK, WIDE), BF16)] * BLOCKS
        out_specs = [whole] * BLOCKS
        scratch = [
            pltpu.VMEM(m_shape, F32),
            pltpu.VMEM(acc_shape, F32),
            *scratch,
            pltpu.VMEM((8 * TOK, 2 * HD), BF16),
            pltpu.VMEM((8 * TOK, HD), BF16),
        ]
    else:
        out_shape = [jax.ShapeDtypeStruct(m_shape, F32), jax.ShapeDtypeStruct(acc_shape, F32)]
        out_specs = [whole] * 2
    return pl.pallas_call(
        functools.partial(attention_kernel, len(shards), first, last),
        grid=(1,),
        out_shape=out_shape,
        in_specs=specs,
        out_specs=out_specs,
        scratch_shapes=scratch,
        compiler_params=pltpu.CompilerParams(vmem_limit_bytes=56 * 2**20),
        cost_estimate=pl.CostEstimate(flops=1, bytes_accessed=1, transcendentals=1),
        name="attention",
    )(*args)


def merge_kernel(*refs):
    parts, out_ref = refs[:BLOCKS], refs[BLOCKS]
    stats = []
    for b in range(BLOCKS):
        lanes = parts[b][:, QPH * HD : WIDE].astype(F32)
        stats.append(lanes[:, 0:8] + lanes[:, 8:16] + lanes[:, 16:24])
    top = functools.reduce(jnp.maximum, stats)
    shares = [jnp.exp2(s - top) for s in stats]
    whole = functools.reduce(jnp.add, shares)
    shares = [s / whole for s in shares]
    for h in range(QPH):
        cols = slice(h * HD, (h + 1) * HD)
        out_ref[:, cols] = functools.reduce(
            jnp.add,
            [parts[b][:, cols].astype(F32) * shares[b][:, h : h + 1] for b in range(BLOCKS)],
        ).astype(BF16)


def merge(parts):
    return pl.pallas_call(
        merge_kernel,
        out_shape=jax.ShapeDtypeStruct((TOK, QPH * HD), BF16),
        name="merge",
    )(*parts)


def product_kernel(place_ref, *refs):
    blocks, weights, out_ref, every = refs[:8], refs[8:12], refs[12], refs[13]
    z, yc = place_ref[0], place_ref[1]
    for k in range(Z):
        every[(z + k) % Z] = blocks[k][...]
    rows = every[...].reshape(Z * TOK, QPH * HD)
    for r in range(YC):
        part = jnp.dot(rows, weights[r][...], preferred_element_type=F32)
        out_ref[:, yc ^ r] = part.astype(BF16).reshape(Z, TOK, 256)


def product(place, blocks, weights):
    whole = pl.BlockSpec(memory_space=pltpu.VMEM)
    return pl.pallas_call(
        product_kernel,
        out_shape=jax.ShapeDtypeStruct((Z, YC, TOK, 256), BF16),
        in_specs=[pl.BlockSpec(memory_space=pltpu.SMEM)] + [whole] * 12,
        out_specs=whole,
        scratch_shapes=[pltpu.VMEM((Z, TOK, QPH * HD), BF16)],
        compiler_params=pltpu.CompilerParams(vmem_limit_bytes=56 * 2**20),
        name="product",
    )(place, *blocks, *weights)


def body(queries, cache_keys, cache_values, new_keys, new_values, cache_len, span_rank, out_weight):
    seq = lax.axis_index("seq")
    z, yc = seq // YC, seq % YC

    own = pack(cache_len, cache_keys, cache_values, new_keys, new_values)
    over_c = lambda v: seq_permute(v, lambda z, y, c: (z, y, 1 - c))
    over_y = lambda v: seq_permute(v, lambda z, y, c: (z, 1 - y, c))
    shift = lambda v, n: seq_permute(v, lambda z, y, c: (z + n, y, c))

    own_pair = (own, over_c(own))
    q_far, q_side = shift(queries, 4), over_y(queries)
    kv_up, kv_down = shift(own, -1), shift(own, 1)
    q_cross = over_y(q_far)
    sent, q_cross = lax.optimization_barrier((own, q_cross))
    kv_two = seq_permute(sent, lambda z, y, c: (z - 2 if z % 2 == 0 else z + 2, y, c))
    q_blocks = (q_cross, q_far, q_side, queries)

    ranks = span_rank.reshape(Z, YC, TOK)
    two = jnp.where(z % 2 == 0, z + 2, z - 2)
    near = ranks[jnp.stack([z, z + 1, z - 1, two]) % Z]
    k_rank = near[:, jnp.stack([yc, yc ^ 1])].reshape(8 * TOK, 1)
    k_rank = jnp.broadcast_to(k_rank, (8 * TOK, HD))
    both = ranks[jnp.stack([z + 4, z]) % Z]
    q_rank = both[:, jnp.stack([yc ^ 2, yc])].reshape(BLOCKS, TOK)
    q_rank = jnp.tile(q_rank, (1, QPH)).reshape(1, BLOCKS * ROWS)

    state = attention(q_blocks, own_pair)
    kv_up, kv_down, *state = lax.optimization_barrier((kv_up, kv_down, *state))
    next_pairs = (kv_up, over_c(kv_up), kv_down, over_c(kv_down))
    weight = lax.optimization_barrier((out_weight, kv_up, kv_down))[0]
    weight_y = over_y(weight)
    weights = [out_weight, over_c(weight), weight_y, over_c(weight_y)]
    state = attention(q_blocks, next_pairs, state)
    kv_two, *state = lax.optimization_barrier((kv_two, *state))
    last_pair = (kv_two, over_c(kv_two))
    new = (*own_pair, *next_pairs, *last_pair)
    cross, far, side, mine = attention(q_blocks, last_pair, state, new, q_rank, k_rank)
    cross = seq_permute(cross, lambda z, y, c: (z + 4, 1 - y, c))
    attended = merge((cross, shift(far, 4), over_y(side), mine))

    blocks = [None] * Z
    blocks[0] = attended
    for k in (1, 2, 3):
        blocks[k] = shift(blocks[k - 1], -1)
        blocks[Z - k] = shift(blocks[(Z - k + 1) % Z], 1)
    blocks[4] = shift(blocks[3], -1)
    shares = product(jnp.stack([z, yc]), blocks, weights)
    shares = lax.all_to_all(shares, "head", 0, 0, tiled=True)
    projected = jnp.sum(shares.astype(F32), axis=0).astype(BF16)
    projected = lax.all_to_all(projected, "seq", 0, 0, axis_index_groups=PLANES, tiled=True)
    return projected.reshape(YC * TOK, 256)


def solution(mesh):
    return jax.shard_map(
        body,
        mesh=mesh,
        in_specs=(
            P("seq", "head"),
            P("head", "seq", None),
            P("head", "seq", None),
            P("seq", "head"),
            P("seq", "head"),
            P("seq"),
            P(),
            P("head", "seq"),
        ),
        out_specs=P("head", "seq"),
        check_vma=False,
    )
```

```python
import functools
import math

import jax
import jax.numpy as jnp
from jax import lax
from jax.experimental import pallas as pl
from jax.experimental.pallas import tpu as pltpu
from jax.sharding import PartitionSpec as P

NEG_FILL = -1e30
BF16 = jnp.bfloat16
F32 = jnp.float32
Z, YC = 8, 4
QPH, HD = 8, 128
TOK = 64
CACHE = 1024
GRAN = 128
CHUNK = 512
BLOCKS = 4
ROWS = TOK * QPH
TILE = 2 * ROWS
VROWS = 144
WIDE = QPH * HD + 128
KEY_AT = 2 * TOK
VALUE_AT = KEY_AT + CACHE
META_AT = VALUE_AT + CACHE
BLOCK_ROWS = META_AT + 16
PLANES = [[z * YC + i for i in range(YC)] for z in range(Z)]


def seq_permute(value, move):
    pairs = []
    for z in range(Z):
        for y in range(2):
            for c in range(2):
                to_z, to_y, to_c = move(z, y, c)
                pairs.append((z * 4 + y * 2 + c, (to_z % Z) * 4 + to_y * 2 + to_c))
    return lax.ppermute(value, "seq", pairs)


def pack_kernel(length_ref, k_ref, v_ref, nk_ref, nv_ref, out_ref):
    length = length_ref[0]
    out_ref[0:TOK, :] = nk_ref[...]
    out_ref[TOK:KEY_AT, :] = nv_ref[...]
    out_ref[KEY_AT:VALUE_AT, :] = k_ref[0]
    out_ref[VALUE_AT:META_AT, :] = v_ref[0]
    row = lax.broadcasted_iota(jnp.int32, (16, HD), 0)
    meta = jnp.where(row < 8, length // 32, length % 32)
    out_ref[META_AT:BLOCK_ROWS, :] = meta.astype(F32).astype(BF16)


def pack(length, keys, values, new_keys, new_values):
    whole = pl.BlockSpec(memory_space=pltpu.VMEM)
    return pl.pallas_call(
        pack_kernel,
        out_shape=jax.ShapeDtypeStruct((BLOCK_ROWS, HD), BF16),
        in_specs=[pl.BlockSpec(memory_space=pltpu.SMEM)] + [whole] * 4,
        out_specs=whole,
        name="pack",
    )(length, keys, values, new_keys, new_values)


def attention_kernel(shards, first, last, *refs):
    refs = list(refs)
    take = lambda n: [refs.pop(0) for _ in range(n)]
    q_refs, shard_refs = take(BLOCKS), take(shards)
    if not first:
        m_in, acc_in = take(2)
    if last:
        new_refs = take(8)
        q_rank, k_rank = take(2)
        out_refs = take(BLOCKS)
    m_all, acc = take(2)
    q_all, k_all, v_all, s0, s1, p0, p1, scale0, scale1 = take(9)
    if last:
        new_k, new_v = take(2)
    factor = F32(math.log2(math.e) / math.sqrt(HD))
    for b in range(BLOCKS):
        for h in range(QPH):
            scaled = q_refs[b][:, h * HD : (h + 1) * HD].astype(F32) * factor
            high = scaled.astype(BF16)
            rows = pl.ds(b * ROWS + h * TOK, TOK)
            q_all[rows, 0:HD] = high
            q_all[rows, HD : 2 * HD] = (scaled - high.astype(F32)).astype(BF16)
    if first:
        m_all[...] = jnp.full(m_all.shape, NEG_FILL, F32)
        acc[...] = jnp.zeros(acc.shape, F32)
    else:
        m_all[...] = m_in[...]
        acc[...] = acc_in[...]

    position = lax.broadcasted_iota(jnp.int32, (CACHE, HD), 0)
    lane_position = lax.broadcasted_iota(jnp.int32, (16, CACHE), 1)
    row16 = lax.broadcasted_iota(jnp.int32, (16, CACHE), 0)
    lengths = []
    for ref in shard_refs:
        meta = ref[META_AT:BLOCK_ROWS, :].astype(F32)
        lengths.append(jnp.max(meta[0:8, :] * 32.0 + meta[8:16, :]).astype(jnp.int32))
    total = jnp.int32(0)
    for ref, length in zip(shard_refs, lengths):
        start = pl.multiple_of(total, GRAN)
        counted = position < length
        keys = ref[KEY_AT:VALUE_AT, :]
        keys = jnp.where(counted, keys, jnp.broadcast_to(keys[0:1, :], keys.shape))
        k_all[pl.ds(start, CACHE), 0:HD] = keys
        k_all[pl.ds(start, CACHE), HD : 2 * HD] = keys
        values = ref[VALUE_AT:META_AT, :]
        values = jnp.where(counted, values, jnp.zeros_like(values))
        v_all[0:HD, pl.ds(start, CACHE)] = values.T
        flags = jnp.logical_and(lane_position < length, row16 == 0)
        v_all[HD:VROWS, pl.ds(start, CACHE)] = jnp.where(flags, 1.0, 0.0).astype(BF16)
        total = total + ((length + GRAN - 1) // GRAN) * GRAN
    filler = pl.ds(pl.multiple_of(total, GRAN), CHUNK)
    k_all[filler, :] = jnp.broadcast_to(k_all[0:1, :], (CHUNK, 2 * HD))
    v_all[:, filler] = jnp.zeros((VROWS, CHUNK), BF16)

    left, right = slice(0, TILE), slice(TILE, 2 * TILE)

    def scores(s, k, rows):
        s[...] = lax.dot_general(
            k, q_all[rows, :], (((1,), (1,)), ((), ())), preferred_element_type=F32
        )

    def weigh(s, p, scale, rows):
        before = m_all[:, rows]
        top = jnp.maximum(before, jnp.max(s, axis=0, keepdims=True))
        m_all[:, rows] = top
        p[...] = jnp.exp2(s - top).astype(BF16)
        scale[...] = jnp.exp2(before - top)

    def add(p, scale, v, rows):
        acc[:, rows] = acc[:, rows] * scale[...] + jnp.dot(
            v, p[...], preferred_element_type=F32
        )

    def chunk(i):
        return pl.ds(pl.multiple_of(i * CHUNK, CHUNK), CHUNK)

    count = (total + CHUNK - 1) // CHUNK
    p1[...] = jnp.zeros(p1.shape, BF16)
    scale1[...] = jnp.ones(scale1.shape, F32)
    scores(s0, k_all[0:CHUNK, :], left)

    @pl.loop(0, count)
    def _(i):
        before, here = chunk(jnp.maximum(i - 1, 0)), chunk(i)
        after = chunk(jnp.minimum(i + 1, count - 1))
        scores(s1, k_all[here, :], right)
        weigh(s0[...], p0, scale0, left)
        add(p1, scale1, v_all[:, before], right)
        scores(s0, k_all[after, :], left)
        weigh(s1[...], p1, scale1, right)
        add(p0, scale0, v_all[:, here], left)

    add(p1, scale1, v_all[:, chunk(count - 1)], right)
    if not last:
        return
    for s in range(8):
        rows = pl.ds(s * TOK, TOK)
        fresh = new_refs[s][0:TOK, :]
        new_k[rows, 0:HD] = fresh
        new_k[rows, HD : 2 * HD] = fresh
        new_v[rows, :] = new_refs[s][TOK : 2 * TOK, :]
    ones16 = jnp.where(row16[:, 0:CHUNK] == 0, 1.0, 0.0).astype(BF16)
    values = jnp.concatenate([new_v[...].T, ones16], axis=0)
    scores(s0, new_k[...], left)
    scores(s1, new_k[...], right)
    ranks = k_rank[:, 0:1]
    weigh(jnp.where(ranks <= q_rank[:, left], s0[...], NEG_FILL), p0, scale0, left)
    add(p0, scale0, values, left)
    weigh(jnp.where(ranks <= q_rank[:, right], s1[...], NEG_FILL), p1, scale1, right)
    add(p1, scale1, values, right)
    for b in range(BLOCKS):
        stats = []
        for h in range(QPH):
            cols = slice(b * ROWS + h * TOK, b * ROWS + (h + 1) * TOK)
            held = acc[:, cols]
            weight = held[HD : HD + 1, :]
            out_refs[b][:, h * HD : (h + 1) * HD] = (held[0:HD, :] / weight).T.astype(BF16)
            stats.append(m_all[:, cols] + jnp.log2(weight))
        stats = jnp.concatenate(stats, axis=0)
        high = stats.astype(BF16).astype(F32)
        middle = (stats - high).astype(BF16).astype(F32)
        low = stats - high - middle
        stats = jnp.concatenate([high, middle, low, jnp.zeros((104, TOK), F32)], axis=0)
        out_refs[b][:, QPH * HD : WIDE] = stats.T.astype(BF16)


def attention(q_blocks, shards, state=None, new=None, q_rank=None, k_rank=None):
    first, last = state is None, new is not None
    m_shape, acc_shape = (1, BLOCKS * ROWS), (VROWS, BLOCKS * ROWS)
    args = [*q_blocks, *shards]
    whole = pl.BlockSpec(memory_space=pltpu.VMEM)
    specs = [whole] * len(args)
    if not first:
        args += state
        specs += [whole] * 2
    keys = len(shards) * CACHE + CHUNK
    scratch = [
        pltpu.VMEM((BLOCKS * ROWS, 2 * HD), BF16),
        pltpu.VMEM((keys, 2 * HD), BF16),
        pltpu.VMEM((VROWS, keys), BF16),
        pltpu.VMEM((CHUNK, TILE), F32),
        pltpu.VMEM((CHUNK, TILE), F32),
        pltpu.VMEM((CHUNK, TILE), BF16),
        pltpu.VMEM((CHUNK, TILE), BF16),
        pltpu.VMEM((1, TILE), F32),
        pltpu.VMEM((1, TILE), F32),
    ]
    if last:
        args += [*new, q_rank, k_rank]
        specs += [pl.BlockSpec((2 * TOK, HD), lambda i: (0, 0))] * 8 + [whole] * 2
        out_shape = [jax.ShapeDtypeStruct((TOK, WIDE), BF16)] * BLOCKS
        out_specs = [whole] * BLOCKS
        scratch = [
            pltpu.VMEM(m_shape, F32),
            pltpu.VMEM(acc_shape, F32),
            *scratch,
            pltpu.VMEM((8 * TOK, 2 * HD), BF16),
            pltpu.VMEM((8 * TOK, HD), BF16),
        ]
    else:
        out_shape = [jax.ShapeDtypeStruct(m_shape, F32), jax.ShapeDtypeStruct(acc_shape, F32)]
        out_specs = [whole] * 2
    return pl.pallas_call(
        functools.partial(attention_kernel, len(shards), first, last),
        grid=(1,),
        out_shape=out_shape,
        in_specs=specs,
        out_specs=out_specs,
        scratch_shapes=scratch,
        compiler_params=pltpu.CompilerParams(vmem_limit_bytes=56 * 2**20),
        cost_estimate=pl.CostEstimate(flops=1, bytes_accessed=1, transcendentals=1),
        name="attention",
    )(*args)


def merge_kernel(*refs):
    parts, out_ref = refs[:BLOCKS], refs[BLOCKS]
    stats = []
    for b in range(BLOCKS):
        lanes = parts[b][:, QPH * HD : WIDE].astype(F32)
        stats.append(lanes[:, 0:8] + lanes[:, 8:16] + lanes[:, 16:24])
    top = functools.reduce(jnp.maximum, stats)
    shares = [jnp.exp2(s - top) for s in stats]
    whole = functools.reduce(jnp.add, shares)
    shares = [s / whole for s in shares]
    for h in range(QPH):
        cols = slice(h * HD, (h + 1) * HD)
        out_ref[:, cols] = functools.reduce(
            jnp.add,
            [parts[b][:, cols].astype(F32) * shares[b][:, h : h + 1] for b in range(BLOCKS)],
        ).astype(BF16)


def merge(parts):
    return pl.pallas_call(
        merge_kernel,
        out_shape=jax.ShapeDtypeStruct((TOK, QPH * HD), BF16),
        name="merge",
    )(*parts)


def product_kernel(place_ref, *refs):
    blocks, weights, out_ref, every = refs[:8], refs[8:12], refs[12], refs[13]
    z, yc = place_ref[0], place_ref[1]
    for k in range(Z):
        every[(z + k) % Z] = blocks[k][...]
    rows = every[...].reshape(Z * TOK, QPH * HD)
    for r in range(YC):
        part = jnp.dot(rows, weights[r][...], preferred_element_type=F32)
        out_ref[:, yc ^ r] = part.astype(BF16).reshape(Z, TOK, 256)


def product(place, blocks, weights):
    whole = pl.BlockSpec(memory_space=pltpu.VMEM)
    return pl.pallas_call(
        product_kernel,
        out_shape=jax.ShapeDtypeStruct((Z, YC, TOK, 256), BF16),
        in_specs=[pl.BlockSpec(memory_space=pltpu.SMEM)] + [whole] * 12,
        out_specs=whole,
        scratch_shapes=[pltpu.VMEM((Z, TOK, QPH * HD), BF16)],
        compiler_params=pltpu.CompilerParams(vmem_limit_bytes=56 * 2**20),
        name="product",
    )(place, *blocks, *weights)


def body(queries, cache_keys, cache_values, new_keys, new_values, cache_len, span_rank, out_weight):
    seq = lax.axis_index("seq")
    z, yc = seq // YC, seq % YC

    own = pack(cache_len, cache_keys, cache_values, new_keys, new_values)
    over_c = lambda v: seq_permute(v, lambda z, y, c: (z, y, 1 - c))
    over_y = lambda v: seq_permute(v, lambda z, y, c: (z, 1 - y, c))
    shift = lambda v, n: seq_permute(v, lambda z, y, c: (z + n, y, c))

    q_far, q_side = shift(queries, 4), over_y(queries)
    own_pair = (own, over_c(own))
    sent, q_far = lax.optimization_barrier((own, q_far))
    kv_up, kv_down = shift(sent, -1), shift(sent, 1)
    q_cross = over_y(q_far)
    sent, q_cross = lax.optimization_barrier((own, q_cross))
    kv_two = seq_permute(sent, lambda z, y, c: (z - 2 if z % 2 == 0 else z + 2, y, c))
    q_blocks = (q_cross, q_far, q_side, queries)

    ranks = span_rank.reshape(Z, YC, TOK)
    two = jnp.where(z % 2 == 0, z + 2, z - 2)
    near = ranks[jnp.stack([z, z + 1, z - 1, two]) % Z]
    k_rank = near[:, jnp.stack([yc, yc ^ 1])].reshape(8 * TOK, 1)
    k_rank = jnp.broadcast_to(k_rank, (8 * TOK, HD))
    both = ranks[jnp.stack([z + 4, z]) % Z]
    q_rank = both[:, jnp.stack([yc ^ 2, yc])].reshape(BLOCKS, TOK)
    q_rank = jnp.tile(q_rank, (1, QPH)).reshape(1, BLOCKS * ROWS)

    q_rank, k_rank, own = lax.optimization_barrier((q_rank, k_rank, own))
    own_pair = (own, own_pair[1])
    state = attention(q_blocks, own_pair)
    kv_up, kv_down, *state = lax.optimization_barrier((kv_up, kv_down, *state))
    next_pairs = (kv_up, over_c(kv_up), kv_down, over_c(kv_down))
    weight = lax.optimization_barrier((out_weight, kv_up, kv_down))[0]
    weight_y = over_y(weight)
    weights = [out_weight, over_c(weight), weight_y, over_c(weight_y)]
    state = attention(q_blocks, next_pairs, state)
    kv_two, *state = lax.optimization_barrier((kv_two, *state))
    last_pair = (kv_two, over_c(kv_two))
    new = (*own_pair, *next_pairs, *last_pair)
    cross, far, side, mine = attention(q_blocks, last_pair, state, new, q_rank, k_rank)
    cross = seq_permute(cross, lambda z, y, c: (z + 4, 1 - y, c))
    attended = merge((cross, shift(far, 4), over_y(side), mine))

    blocks = [None] * Z
    blocks[0] = attended
    for k in (1, 2, 3):
        blocks[k] = shift(blocks[k - 1], -1)
        blocks[Z - k] = shift(blocks[(Z - k + 1) % Z], 1)
    blocks[4] = shift(blocks[3], -1)
    shares = product(jnp.stack([z, yc]), blocks, weights)
    shares = lax.all_to_all(shares, "head", 0, 0, tiled=True)
    projected = jnp.sum(shares.astype(F32), axis=0).astype(BF16)
    projected = lax.all_to_all(projected, "seq", 0, 0, axis_index_groups=PLANES, tiled=True)
    return projected.reshape(YC * TOK, 256)


def solution(mesh):
    return jax.shard_map(
        body,
        mesh=mesh,
        in_specs=(
            P("seq", "head"),
            P("head", "seq", None),
            P("head", "seq", None),
            P("seq", "head"),
            P("seq", "head"),
            P("seq"),
            P(),
            P("head", "seq"),
        ),
        out_specs=P("head", "seq"),
        check_vma=False,
    )
```

```python
import functools
import math

import jax
import jax.numpy as jnp
from jax import lax
from jax.experimental import pallas as pl
from jax.experimental.pallas import tpu as pltpu
from jax.sharding import PartitionSpec as P

NEG_FILL = -1e30
BF16 = jnp.bfloat16
F32 = jnp.float32
Z, YC = 8, 4
QPH, HD = 8, 128
TOK = 64
CACHE = 1024
GRAN = 128
CHUNK = 512
BLOCKS = 4
ROWS = TOK * QPH
TILE = 2 * ROWS
VROWS = 144
WIDE = QPH * HD + 128
KEY_AT = 2 * TOK
VALUE_AT = KEY_AT + CACHE
META_AT = VALUE_AT + CACHE
BLOCK_ROWS = META_AT + 16
PLANES = [[z * YC + i for i in range(YC)] for z in range(Z)]


def seq_permute(value, move):
    pairs = []
    for z in range(Z):
        for y in range(2):
            for c in range(2):
                to_z, to_y, to_c = move(z, y, c)
                pairs.append((z * 4 + y * 2 + c, (to_z % Z) * 4 + to_y * 2 + to_c))
    return lax.ppermute(value, "seq", pairs)


def pack_kernel(length_ref, k_ref, v_ref, nk_ref, nv_ref, out_ref):
    length = length_ref[0]
    out_ref[0:TOK, :] = nk_ref[...]
    out_ref[TOK:KEY_AT, :] = nv_ref[...]
    out_ref[KEY_AT:VALUE_AT, :] = k_ref[0]
    out_ref[VALUE_AT:META_AT, :] = v_ref[0]
    row = lax.broadcasted_iota(jnp.int32, (16, HD), 0)
    meta = jnp.where(row < 8, length // 32, length % 32)
    out_ref[META_AT:BLOCK_ROWS, :] = meta.astype(F32).astype(BF16)


def pack(length, keys, values, new_keys, new_values):
    whole = pl.BlockSpec(memory_space=pltpu.VMEM)
    return pl.pallas_call(
        pack_kernel,
        out_shape=jax.ShapeDtypeStruct((BLOCK_ROWS, HD), BF16),
        in_specs=[pl.BlockSpec(memory_space=pltpu.SMEM)] + [whole] * 4,
        out_specs=whole,
        name="pack",
    )(length, keys, values, new_keys, new_values)


def attention_kernel(shards, first, last, *refs):
    refs = list(refs)
    take = lambda n: [refs.pop(0) for _ in range(n)]
    q_refs, shard_refs = take(BLOCKS), take(shards)
    if not first:
        m_in, acc_in = take(2)
    if last:
        new_refs = take(8)
        ids, span = take(2)
        out_refs = take(BLOCKS)
    m_all, acc = take(2)
    q_all, k_all, v_all, s0, s1, p0, p1, scale0, scale1 = take(9)
    if last:
        new_k, new_v = take(2)
    factor = F32(math.log2(math.e) / math.sqrt(HD))
    for b in range(BLOCKS):
        for h in range(QPH):
            scaled = q_refs[b][:, h * HD : (h + 1) * HD].astype(F32) * factor
            high = scaled.astype(BF16)
            rows = pl.ds(b * ROWS + h * TOK, TOK)
            q_all[rows, 0:HD] = high
            q_all[rows, HD : 2 * HD] = (scaled - high.astype(F32)).astype(BF16)
    if first:
        m_all[...] = jnp.full(m_all.shape, NEG_FILL, F32)
        acc[...] = jnp.zeros(acc.shape, F32)
    else:
        m_all[...] = m_in[...]
        acc[...] = acc_in[...]

    position = lax.broadcasted_iota(jnp.int32, (CACHE, HD), 0)
    lane_position = lax.broadcasted_iota(jnp.int32, (16, CACHE), 1)
    row16 = lax.broadcasted_iota(jnp.int32, (16, CACHE), 0)
    lengths = []
    for ref in shard_refs:
        meta = ref[META_AT:BLOCK_ROWS, :].astype(F32)
        lengths.append(jnp.max(meta[0:8, :] * 32.0 + meta[8:16, :]).astype(jnp.int32))
    total = jnp.int32(0)
    for ref, length in zip(shard_refs, lengths):
        start = pl.multiple_of(total, GRAN)
        counted = position < length
        keys = ref[KEY_AT:VALUE_AT, :]
        keys = jnp.where(counted, keys, jnp.broadcast_to(keys[0:1, :], keys.shape))
        k_all[pl.ds(start, CACHE), 0:HD] = keys
        k_all[pl.ds(start, CACHE), HD : 2 * HD] = keys
        values = ref[VALUE_AT:META_AT, :]
        values = jnp.where(counted, values, jnp.zeros_like(values))
        v_all[0:HD, pl.ds(start, CACHE)] = values.T
        flags = jnp.logical_and(lane_position < length, row16 == 0)
        v_all[HD:VROWS, pl.ds(start, CACHE)] = jnp.where(flags, 1.0, 0.0).astype(BF16)
        total = total + ((length + GRAN - 1) // GRAN) * GRAN
    filler = pl.ds(pl.multiple_of(total, GRAN), CHUNK)
    k_all[filler, :] = jnp.broadcast_to(k_all[0:1, :], (CHUNK, 2 * HD))
    v_all[:, filler] = jnp.zeros((VROWS, CHUNK), BF16)

    left, right = slice(0, TILE), slice(TILE, 2 * TILE)

    def scores(s, k, rows):
        s[...] = lax.dot_general(
            k, q_all[rows, :], (((1,), (1,)), ((), ())), preferred_element_type=F32
        )

    def weigh(s, p, scale, rows):
        before = m_all[:, rows]
        top = jnp.maximum(before, jnp.max(s, axis=0, keepdims=True))
        m_all[:, rows] = top
        p[...] = jnp.exp2(s - top).astype(BF16)
        scale[...] = jnp.exp2(before - top)

    def add(p, scale, v, rows):
        acc[:, rows] = acc[:, rows] * scale[...] + jnp.dot(
            v, p[...], preferred_element_type=F32
        )

    def chunk(i):
        return pl.ds(pl.multiple_of(i * CHUNK, CHUNK), CHUNK)

    count = (total + CHUNK - 1) // CHUNK
    p1[...] = jnp.zeros(p1.shape, BF16)
    scale1[...] = jnp.ones(scale1.shape, F32)
    scores(s0, k_all[0:CHUNK, :], left)

    @pl.loop(0, count)
    def _(i):
        before, here = chunk(jnp.maximum(i - 1, 0)), chunk(i)
        after = chunk(jnp.minimum(i + 1, count - 1))
        scores(s1, k_all[here, :], right)
        weigh(s0[...], p0, scale0, left)
        add(p1, scale1, v_all[:, before], right)
        scores(s0, k_all[after, :], left)
        weigh(s1[...], p1, scale1, right)
        add(p0, scale0, v_all[:, here], left)

    add(p1, scale1, v_all[:, chunk(count - 1)], right)
    if not last:
        return
    for s in range(8):
        rows = pl.ds(s * TOK, TOK)
        fresh = new_refs[s][0:TOK, :]
        new_k[rows, 0:HD] = fresh
        new_k[rows, HD : 2 * HD] = fresh
        new_v[rows, :] = new_refs[s][TOK : 2 * TOK, :]
    ones16 = jnp.where(row16[:, 0:CHUNK] == 0, 1.0, 0.0).astype(BF16)
    values = jnp.concatenate([new_v[...].T, ones16], axis=0)
    scores(s0, new_k[...], left)
    scores(s1, new_k[...], right)

    def rank(i):
        return span[pl.ds(ids[i], 1), :].astype(F32)

    q_rank = jnp.concatenate([rank(b) for b in range(BLOCKS) for _ in range(QPH)], axis=1)
    k_rank = jnp.concatenate([rank(BLOCKS + s) for s in range(8)], axis=0)
    k_rank = jnp.concatenate([k_rank, jnp.zeros((8, HD - TOK), F32)], axis=1).T
    ranks = jnp.concatenate([k_rank[0:TOK, s : s + 1] for s in range(8)], axis=0)
    weigh(jnp.where(ranks <= q_rank[:, left], s0[...], NEG_FILL), p0, scale0, left)
    add(p0, scale0, values, left)
    weigh(jnp.where(ranks <= q_rank[:, right], s1[...], NEG_FILL), p1, scale1, right)
    add(p1, scale1, values, right)
    for b in range(BLOCKS):
        stats = []
        for h in range(QPH):
            cols = slice(b * ROWS + h * TOK, b * ROWS + (h + 1) * TOK)
            held = acc[:, cols]
            weight = held[HD : HD + 1, :]
            out_refs[b][:, h * HD : (h + 1) * HD] = (held[0:HD, :] / weight).T.astype(BF16)
            stats.append(m_all[:, cols] + jnp.log2(weight))
        stats = jnp.concatenate(stats, axis=0)
        high = stats.astype(BF16).astype(F32)
        middle = (stats - high).astype(BF16).astype(F32)
        low = stats - high - middle
        stats = jnp.concatenate([high, middle, low, jnp.zeros((104, TOK), F32)], axis=0)
        out_refs[b][:, QPH * HD : WIDE] = stats.T.astype(BF16)


def attention(q_blocks, shards, state=None, new=None, ids=None, span=None):
    first, last = state is None, new is not None
    m_shape, acc_shape = (1, BLOCKS * ROWS), (VROWS, BLOCKS * ROWS)
    args = [*q_blocks, *shards]
    whole = pl.BlockSpec(memory_space=pltpu.VMEM)
    specs = [whole] * len(args)
    if not first:
        args += state
        specs += [whole] * 2
    keys = len(shards) * CACHE + CHUNK
    scratch = [
        pltpu.VMEM((BLOCKS * ROWS, 2 * HD), BF16),
        pltpu.VMEM((keys, 2 * HD), BF16),
        pltpu.VMEM((VROWS, keys), BF16),
        pltpu.VMEM((CHUNK, TILE), F32),
        pltpu.VMEM((CHUNK, TILE), F32),
        pltpu.VMEM((CHUNK, TILE), BF16),
        pltpu.VMEM((CHUNK, TILE), BF16),
        pltpu.VMEM((1, TILE), F32),
        pltpu.VMEM((1, TILE), F32),
    ]
    if last:
        args += [*new, ids, span]
        specs += [pl.BlockSpec((2 * TOK, HD), lambda i: (0, 0))] * 8
        specs += [pl.BlockSpec(memory_space=pltpu.SMEM), whole]
        out_shape = [jax.ShapeDtypeStruct((TOK, WIDE), BF16)] * BLOCKS
        out_specs = [whole] * BLOCKS
        scratch = [
            pltpu.VMEM(m_shape, F32),
            pltpu.VMEM(acc_shape, F32),
            *scratch,
            pltpu.VMEM((8 * TOK, 2 * HD), BF16),
            pltpu.VMEM((8 * TOK, HD), BF16),
        ]
    else:
        out_shape = [jax.ShapeDtypeStruct(m_shape, F32), jax.ShapeDtypeStruct(acc_shape, F32)]
        out_specs = [whole] * 2
    return pl.pallas_call(
        functools.partial(attention_kernel, len(shards), first, last),
        grid=(1,),
        out_shape=out_shape,
        in_specs=specs,
        out_specs=out_specs,
        scratch_shapes=scratch,
        compiler_params=pltpu.CompilerParams(vmem_limit_bytes=56 * 2**20),
        cost_estimate=pl.CostEstimate(flops=1, bytes_accessed=1, transcendentals=1),
        name="attention",
    )(*args)


def merge_kernel(*refs):
    parts, out_ref = refs[:BLOCKS], refs[BLOCKS]
    stats = []
    for b in range(BLOCKS):
        lanes = parts[b][:, QPH * HD : WIDE].astype(F32)
        stats.append(lanes[:, 0:8] + lanes[:, 8:16] + lanes[:, 16:24])
    top = functools.reduce(jnp.maximum, stats)
    shares = [jnp.exp2(s - top) for s in stats]
    whole = functools.reduce(jnp.add, shares)
    shares = [s / whole for s in shares]
    for h in range(QPH):
        cols = slice(h * HD, (h + 1) * HD)
        out_ref[:, cols] = functools.reduce(
            jnp.add,
            [parts[b][:, cols].astype(F32) * shares[b][:, h : h + 1] for b in range(BLOCKS)],
        ).astype(BF16)


def merge(parts):
    return pl.pallas_call(
        merge_kernel,
        out_shape=jax.ShapeDtypeStruct((TOK, QPH * HD), BF16),
        name="merge",
    )(*parts)


def product_kernel(place_ref, *refs):
    blocks, weights, out_ref, every = refs[:8], refs[8:12], refs[12], refs[13]
    z, yc = place_ref[0], place_ref[1]
    for k in range(Z):
        every[(z + k) % Z] = blocks[k][...]
    rows = every[...].reshape(Z * TOK, QPH * HD)
    for r in range(YC):
        part = jnp.dot(rows, weights[r][...], preferred_element_type=F32)
        out_ref[:, yc ^ r] = part.astype(BF16).reshape(Z, TOK, 256)


def product(place, blocks, weights):
    whole = pl.BlockSpec(memory_space=pltpu.VMEM)
    return pl.pallas_call(
        product_kernel,
        out_shape=jax.ShapeDtypeStruct((Z, YC, TOK, 256), BF16),
        in_specs=[pl.BlockSpec(memory_space=pltpu.SMEM)] + [whole] * 12,
        out_specs=whole,
        scratch_shapes=[pltpu.VMEM((Z, TOK, QPH * HD), BF16)],
        compiler_params=pltpu.CompilerParams(vmem_limit_bytes=56 * 2**20),
        name="product",
    )(place, *blocks, *weights)


def body(queries, cache_keys, cache_values, new_keys, new_values, cache_len, span_rank, out_weight):
    seq = lax.axis_index("seq")
    z, yc = seq // YC, seq % YC

    own = pack(cache_len, cache_keys, cache_values, new_keys, new_values)
    over_c = lambda v: seq_permute(v, lambda z, y, c: (z, y, 1 - c))
    over_y = lambda v: seq_permute(v, lambda z, y, c: (z, 1 - y, c))
    shift = lambda v, n: seq_permute(v, lambda z, y, c: (z + n, y, c))

    q_far, q_side = shift(queries, 4), over_y(queries)
    own_pair = (own, over_c(own))
    sent, q_far = lax.optimization_barrier((own, q_far))
    kv_up, kv_down = shift(sent, -1), shift(sent, 1)
    q_cross = over_y(q_far)
    sent, q_cross = lax.optimization_barrier((own, q_cross))
    kv_two = seq_permute(sent, lambda z, y, c: (z - 2 if z % 2 == 0 else z + 2, y, c))
    q_blocks = (q_cross, q_far, q_side, queries)

    two = jnp.where(z % 2 == 0, z + 2, z + 6)
    row = lambda z, i: z % Z * YC + i
    ids = [row(z + 4, yc ^ 2), row(z + 4, yc), row(z, yc ^ 2), row(z, yc)]
    for n in (z, z + 1, z + 7, two):
        ids += [row(n, yc), row(n, yc ^ 1)]
    ids, span = jnp.stack(ids), span_rank.reshape(Z * YC, TOK)

    state = attention(q_blocks, own_pair)
    kv_up, kv_down, *state = lax.optimization_barrier((kv_up, kv_down, *state))
    next_pairs = (kv_up, over_c(kv_up), kv_down, over_c(kv_down))
    weight = lax.optimization_barrier((out_weight, kv_up, kv_down))[0]
    weight_y, weight_c = over_y(weight), over_c(weight)
    state = attention(q_blocks, next_pairs, state)
    kv_two, weight_y, weight_c, *state = lax.optimization_barrier(
        (kv_two, weight_y, weight_c, *state)
    )
    last_pair = (kv_two, over_c(kv_two))
    weight_yc = over_c(weight_y)
    new = (*own_pair, *next_pairs, *last_pair)
    parts = attention(q_blocks, last_pair, state, new, ids, span)
    weight_yc, cross, far, side, mine = lax.optimization_barrier((weight_yc, *parts))
    weights = [out_weight, weight_c, weight_y, weight_yc]
    cross = seq_permute(cross, lambda z, y, c: (z + 4, 1 - y, c))
    attended = merge((cross, shift(far, 4), over_y(side), mine))

    blocks = [None] * Z
    blocks[0] = attended
    for k in (1, 2, 3):
        blocks[k] = shift(blocks[k - 1], -1)
        blocks[Z - k] = shift(blocks[(Z - k + 1) % Z], 1)
    blocks[4] = shift(blocks[3], -1)
    shares = product(jnp.stack([z, yc]), blocks, weights)
    shares = lax.all_to_all(shares, "head", 0, 0, tiled=True)
    projected = jnp.sum(shares.astype(F32), axis=0).astype(BF16).reshape(YC * TOK, 256)
    return lax.all_to_all(projected, "seq", 0, 0, axis_index_groups=PLANES, tiled=True)


def solution(mesh):
    return jax.shard_map(
        body,
        mesh=mesh,
        in_specs=(
            P("seq", "head"),
            P("head", "seq", None),
            P("head", "seq", None),
            P("seq", "head"),
            P("seq", "head"),
            P("seq"),
            P(),
            P("head", "seq"),
        ),
        out_specs=P("head", "seq"),
        check_vma=False,
    )
```

```python
import functools
import math

import jax
import jax.numpy as jnp
from jax import lax
from jax.experimental import pallas as pl
from jax.experimental.pallas import tpu as pltpu
from jax.sharding import PartitionSpec as P

NEG_FILL = -1e30
BF16 = jnp.bfloat16
F32 = jnp.float32
Z, YC = 8, 4
QPH, HD = 8, 128
TOK = 64
CACHE = 1024
GRAN = 128
CHUNK = 512
BLOCKS = 4
ROWS = TOK * QPH
TILE = 2 * ROWS
VROWS = 144
WIDE = QPH * HD + 128
KEY_AT = 2 * TOK
VALUE_AT = KEY_AT + CACHE
META_AT = VALUE_AT + CACHE
BLOCK_ROWS = META_AT + 16
PLANES = [[z * YC + i for i in range(YC)] for z in range(Z)]


def seq_permute(value, move):
    pairs = []
    for z in range(Z):
        for y in range(2):
            for c in range(2):
                to_z, to_y, to_c = move(z, y, c)
                pairs.append((z * 4 + y * 2 + c, (to_z % Z) * 4 + to_y * 2 + to_c))
    return lax.ppermute(value, "seq", pairs)


def pack_kernel(length_ref, k_ref, v_ref, nk_ref, nv_ref, out_ref):
    length = length_ref[0]
    out_ref[0:TOK, :] = nk_ref[...]
    out_ref[TOK:KEY_AT, :] = nv_ref[...]
    out_ref[KEY_AT:VALUE_AT, :] = k_ref[0]
    out_ref[VALUE_AT:META_AT, :] = v_ref[0]
    row = lax.broadcasted_iota(jnp.int32, (16, HD), 0)
    meta = jnp.where(row < 8, length // 32, length % 32)
    out_ref[META_AT:BLOCK_ROWS, :] = meta.astype(F32).astype(BF16)


def pack(length, keys, values, new_keys, new_values):
    whole = pl.BlockSpec(memory_space=pltpu.VMEM)
    return pl.pallas_call(
        pack_kernel,
        out_shape=jax.ShapeDtypeStruct((BLOCK_ROWS, HD), BF16),
        in_specs=[pl.BlockSpec(memory_space=pltpu.SMEM)] + [whole] * 4,
        out_specs=whole,
        name="pack",
    )(length, keys, values, new_keys, new_values)


def attention_kernel(shards, first, last, *refs):
    refs = list(refs)
    take = lambda n: [refs.pop(0) for _ in range(n)]
    q_refs, shard_refs = take(BLOCKS), take(shards)
    if not first:
        m_in, acc_in = take(2)
    if last:
        new_refs = take(8)
        ids, span = take(2)
        out_refs = take(BLOCKS)
    m_all, acc = take(2)
    q_all, k_all, v_all, s0, s1, p0, p1, scale0, scale1 = take(9)
    if last:
        new_k, new_v = take(2)
    factor = F32(math.log2(math.e) / math.sqrt(HD))
    for b in range(BLOCKS):
        for h in range(QPH):
            scaled = q_refs[b][:, h * HD : (h + 1) * HD].astype(F32) * factor
            high = scaled.astype(BF16)
            rows = pl.ds(b * ROWS + h * TOK, TOK)
            q_all[rows, 0:HD] = high
            q_all[rows, HD : 2 * HD] = (scaled - high.astype(F32)).astype(BF16)
    if first:
        m_all[...] = jnp.full(m_all.shape, NEG_FILL, F32)
        acc[...] = jnp.zeros(acc.shape, F32)
    else:
        m_all[...] = m_in[...]
        acc[...] = acc_in[...]

    position = lax.broadcasted_iota(jnp.int32, (CACHE, HD), 0)
    lane_position = lax.broadcasted_iota(jnp.int32, (16, CACHE), 1)
    row16 = lax.broadcasted_iota(jnp.int32, (16, CACHE), 0)
    lengths = []
    for ref in shard_refs:
        meta = ref[META_AT:BLOCK_ROWS, :].astype(F32)
        lengths.append(jnp.max(meta[0:8, :] * 32.0 + meta[8:16, :]).astype(jnp.int32))
    total = jnp.int32(0)
    for ref, length in zip(shard_refs, lengths):
        start = pl.multiple_of(total, GRAN)
        counted = position < length
        keys = ref[KEY_AT:VALUE_AT, :]
        keys = jnp.where(counted, keys, jnp.broadcast_to(keys[0:1, :], keys.shape))
        k_all[pl.ds(start, CACHE), 0:HD] = keys
        k_all[pl.ds(start, CACHE), HD : 2 * HD] = keys
        values = ref[VALUE_AT:META_AT, :]
        values = jnp.where(counted, values, jnp.zeros_like(values))
        v_all[0:HD, pl.ds(start, CACHE)] = values.T
        flags = jnp.logical_and(lane_position < length, row16 == 0)
        v_all[HD:VROWS, pl.ds(start, CACHE)] = jnp.where(flags, 1.0, 0.0).astype(BF16)
        total = total + ((length + GRAN - 1) // GRAN) * GRAN
    filler = pl.ds(pl.multiple_of(total, GRAN), CHUNK)
    k_all[filler, :] = jnp.broadcast_to(k_all[0:1, :], (CHUNK, 2 * HD))
    v_all[:, filler] = jnp.zeros((VROWS, CHUNK), BF16)

    left, right = slice(0, TILE), slice(TILE, 2 * TILE)

    def scores(s, k, rows):
        s[...] = lax.dot_general(
            k, q_all[rows, :], (((1,), (1,)), ((), ())), preferred_element_type=F32
        )

    def weigh(s, p, scale, rows):
        before = m_all[:, rows]
        top = jnp.maximum(before, jnp.max(s, axis=0, keepdims=True))
        m_all[:, rows] = top
        p[...] = jnp.exp2(s - top).astype(BF16)
        scale[...] = jnp.exp2(before - top)

    def add(p, scale, v, rows):
        acc[:, rows] = acc[:, rows] * scale[...] + jnp.dot(
            v, p[...], preferred_element_type=F32
        )

    def chunk(i):
        return pl.ds(pl.multiple_of(i * CHUNK, CHUNK), CHUNK)

    count = (total + CHUNK - 1) // CHUNK
    p1[...] = jnp.zeros(p1.shape, BF16)
    scale1[...] = jnp.ones(scale1.shape, F32)
    scores(s0, k_all[0:CHUNK, :], left)

    @pl.loop(0, count)
    def _(i):
        before, here = chunk(jnp.maximum(i - 1, 0)), chunk(i)
        after = chunk(jnp.minimum(i + 1, count - 1))
        scores(s1, k_all[here, :], right)
        weigh(s0[...], p0, scale0, left)
        add(p1, scale1, v_all[:, before], right)
        scores(s0, k_all[after, :], left)
        weigh(s1[...], p1, scale1, right)
        add(p0, scale0, v_all[:, here], left)

    add(p1, scale1, v_all[:, chunk(count - 1)], right)
    if not last:
        return
    for s in range(8):
        rows = pl.ds(s * TOK, TOK)
        fresh = new_refs[s][0:TOK, :]
        new_k[rows, 0:HD] = fresh
        new_k[rows, HD : 2 * HD] = fresh
        new_v[rows, :] = new_refs[s][TOK : 2 * TOK, :]
    ones16 = jnp.where(row16[:, 0:CHUNK] == 0, 1.0, 0.0).astype(BF16)
    values = jnp.concatenate([new_v[...].T, ones16], axis=0)
    scores(s0, new_k[...], left)
    scores(s1, new_k[...], right)

    def rank(i):
        return span[pl.ds(ids[i], 1), :].astype(F32)

    q_rank = jnp.concatenate([rank(b) for b in range(BLOCKS) for _ in range(QPH)], axis=1)
    k_rank = jnp.concatenate([rank(BLOCKS + s) for s in range(8)], axis=0)
    k_rank = jnp.concatenate([k_rank, jnp.zeros((8, HD - TOK), F32)], axis=1).T
    ranks = jnp.concatenate([k_rank[0:TOK, s : s + 1] for s in range(8)], axis=0)
    weigh(jnp.where(ranks <= q_rank[:, left], s0[...], NEG_FILL), p0, scale0, left)
    add(p0, scale0, values, left)
    weigh(jnp.where(ranks <= q_rank[:, right], s1[...], NEG_FILL), p1, scale1, right)
    add(p1, scale1, values, right)
    for b in range(BLOCKS):
        stats = []
        for h in range(QPH):
            cols = slice(b * ROWS + h * TOK, b * ROWS + (h + 1) * TOK)
            held = acc[:, cols]
            weight = held[HD : HD + 1, :]
            out_refs[b][:, h * HD : (h + 1) * HD] = (held[0:HD, :] / weight).T.astype(BF16)
            stats.append(m_all[:, cols] + jnp.log2(weight))
        stats = jnp.concatenate(stats, axis=0)
        high = stats.astype(BF16).astype(F32)
        middle = (stats - high).astype(BF16).astype(F32)
        low = stats - high - middle
        stats = jnp.concatenate([high, middle, low, jnp.zeros((104, TOK), F32)], axis=0)
        out_refs[b][:, QPH * HD : WIDE] = stats.T.astype(BF16)


def attention(q_blocks, shards, state=None, new=None, ids=None, span=None):
    first, last = state is None, new is not None
    m_shape, acc_shape = (1, BLOCKS * ROWS), (VROWS, BLOCKS * ROWS)
    args = [*q_blocks, *shards]
    whole = pl.BlockSpec(memory_space=pltpu.VMEM)
    specs = [whole] * len(args)
    if not first:
        args += state
        specs += [whole] * 2
    keys = len(shards) * CACHE + CHUNK
    scratch = [
        pltpu.VMEM((BLOCKS * ROWS, 2 * HD), BF16),
        pltpu.VMEM((keys, 2 * HD), BF16),
        pltpu.VMEM((VROWS, keys), BF16),
        pltpu.VMEM((CHUNK, TILE), F32),
        pltpu.VMEM((CHUNK, TILE), F32),
        pltpu.VMEM((CHUNK, TILE), BF16),
        pltpu.VMEM((CHUNK, TILE), BF16),
        pltpu.VMEM((1, TILE), F32),
        pltpu.VMEM((1, TILE), F32),
    ]
    if last:
        args += [*new, ids, span]
        specs += [pl.BlockSpec((2 * TOK, HD), lambda i: (0, 0))] * 8
        specs += [pl.BlockSpec(memory_space=pltpu.SMEM), whole]
        out_shape = [jax.ShapeDtypeStruct((TOK, WIDE), BF16)] * BLOCKS
        out_specs = [whole] * BLOCKS
        scratch = [
            pltpu.VMEM(m_shape, F32),
            pltpu.VMEM(acc_shape, F32),
            *scratch,
            pltpu.VMEM((8 * TOK, 2 * HD), BF16),
            pltpu.VMEM((8 * TOK, HD), BF16),
        ]
    else:
        out_shape = [jax.ShapeDtypeStruct(m_shape, F32), jax.ShapeDtypeStruct(acc_shape, F32)]
        out_specs = [whole] * 2
    return pl.pallas_call(
        functools.partial(attention_kernel, len(shards), first, last),
        grid=(1,),
        out_shape=out_shape,
        in_specs=specs,
        out_specs=out_specs,
        scratch_shapes=scratch,
        compiler_params=pltpu.CompilerParams(vmem_limit_bytes=56 * 2**20),
        cost_estimate=pl.CostEstimate(flops=1, bytes_accessed=1, transcendentals=1),
        name="attention",
    )(*args)


def merge_kernel(*refs):
    parts, out_ref = refs[:BLOCKS], refs[BLOCKS]
    stats = []
    for b in range(BLOCKS):
        lanes = parts[b][:, QPH * HD : WIDE].astype(F32)
        stats.append(lanes[:, 0:8] + lanes[:, 8:16] + lanes[:, 16:24])
    top = functools.reduce(jnp.maximum, stats)
    shares = [jnp.exp2(s - top) for s in stats]
    whole = functools.reduce(jnp.add, shares)
    shares = [s / whole for s in shares]
    for h in range(QPH):
        cols = slice(h * HD, (h + 1) * HD)
        out_ref[:, cols] = functools.reduce(
            jnp.add,
            [parts[b][:, cols].astype(F32) * shares[b][:, h : h + 1] for b in range(BLOCKS)],
        ).astype(BF16)


def merge(parts):
    return pl.pallas_call(
        merge_kernel,
        out_shape=jax.ShapeDtypeStruct((TOK, QPH * HD), BF16),
        name="merge",
    )(*parts)


def product_kernel(place_ref, *refs):
    blocks, weights, out_ref, every = refs[:8], refs[8:12], refs[12], refs[13]
    z, yc = place_ref[0], place_ref[1]
    for k in range(Z):
        every[(z + k) % Z] = blocks[k][...]
    rows = every[...].reshape(Z * TOK, QPH * HD)
    for r in range(YC):
        part = jnp.dot(rows, weights[r][...], preferred_element_type=F32)
        out_ref[:, yc ^ r] = part.astype(BF16).reshape(Z, TOK, 256)


def product(place, blocks, weights):
    whole = pl.BlockSpec(memory_space=pltpu.VMEM)
    return pl.pallas_call(
        product_kernel,
        out_shape=jax.ShapeDtypeStruct((Z, YC, TOK, 256), BF16),
        in_specs=[pl.BlockSpec(memory_space=pltpu.SMEM)] + [whole] * 12,
        out_specs=whole,
        scratch_shapes=[pltpu.VMEM((Z, TOK, QPH * HD), BF16)],
        compiler_params=pltpu.CompilerParams(vmem_limit_bytes=56 * 2**20),
        name="product",
    )(place, *blocks, *weights)


def body(queries, cache_keys, cache_values, new_keys, new_values, cache_len, span_rank, out_weight):
    seq = lax.axis_index("seq")
    z, yc = seq // YC, seq % YC

    own = pack(cache_len, cache_keys, cache_values, new_keys, new_values)
    over_c = lambda v: seq_permute(v, lambda z, y, c: (z, y, 1 - c))
    over_y = lambda v: seq_permute(v, lambda z, y, c: (z, 1 - y, c))
    shift = lambda v, n: seq_permute(v, lambda z, y, c: (z + n, y, c))

    q_far, q_side = shift(queries, 4), over_y(queries)
    own_pair = (own, over_c(own))
    sent, q_far, q_side = lax.optimization_barrier((own, q_far, q_side))
    kv_up, kv_down = shift(sent, -1), shift(sent, 1)
    q_cross = over_y(q_far)
    sent, q_cross = lax.optimization_barrier((own, q_cross))
    kv_two = seq_permute(sent, lambda z, y, c: (z - 2 if z % 2 == 0 else z + 2, y, c))
    q_blocks = (q_cross, q_far, q_side, queries)

    two = jnp.where(z % 2 == 0, z + 2, z + 6)
    row = lambda z, i: z % Z * YC + i
    ids = [row(z + 4, yc ^ 2), row(z + 4, yc), row(z, yc ^ 2), row(z, yc)]
    for n in (z, z + 1, z + 7, two):
        ids += [row(n, yc), row(n, yc ^ 1)]
    ids, span = jnp.stack(ids), span_rank.reshape(Z * YC, TOK)

    ids, span, own = lax.optimization_barrier((ids, span, own))
    own_pair = (own, own_pair[1])
    state = attention(q_blocks, own_pair)
    kv_up, kv_down, *state = lax.optimization_barrier((kv_up, kv_down, *state))
    next_pairs = (kv_up, over_c(kv_up), kv_down, over_c(kv_down))
    weight = lax.optimization_barrier((out_weight, kv_up, kv_down))[0]
    weight_y = over_y(weight)
    weights = [out_weight, over_c(weight), weight_y, over_c(weight_y)]
    state = attention(q_blocks, next_pairs, state)
    kv_two, *state = lax.optimization_barrier((kv_two, *state))
    last_pair = (kv_two, over_c(kv_two))
    new = (*own_pair, *next_pairs, *last_pair)
    cross, far, side, mine = attention(q_blocks, last_pair, state, new, ids, span)
    cross = seq_permute(cross, lambda z, y, c: (z + 4, 1 - y, c))
    attended = merge((cross, shift(far, 4), over_y(side), mine))

    blocks = [None] * Z
    blocks[0] = attended
    for k in (1, 2, 3):
        blocks[k] = shift(blocks[k - 1], -1)
        blocks[Z - k] = shift(blocks[(Z - k + 1) % Z], 1)
    blocks[4] = shift(blocks[3], -1)
    shares = product(jnp.stack([z, yc]), blocks, weights)
    shares = lax.all_to_all(shares, "head", 0, 0, tiled=True)
    projected = jnp.sum(shares.astype(F32), axis=0).astype(BF16).reshape(YC * TOK, 256)
    return lax.all_to_all(projected, "seq", 0, 0, axis_index_groups=PLANES, tiled=True)


def solution(mesh):
    return jax.shard_map(
        body,
        mesh=mesh,
        in_specs=(
            P("seq", "head"),
            P("head", "seq", None),
            P("head", "seq", None),
            P("seq", "head"),
            P("seq", "head"),
            P("seq"),
            P(),
            P("head", "seq"),
        ),
        out_specs=P("head", "seq"),
        check_vma=False,
    )
```

```python
import functools
import math

import jax
import jax.numpy as jnp
from jax import lax
from jax.experimental import pallas as pl
from jax.experimental.pallas import tpu as pltpu
from jax.sharding import PartitionSpec as P

NEG_FILL = -1e30
BF16 = jnp.bfloat16
F32 = jnp.float32
Z, YC = 8, 4
QPH, HD = 8, 128
TOK = 64
CACHE = 1024
GRAN = 128
CHUNK = 512
BLOCKS = 4
ROWS = TOK * QPH
TILE = 2 * ROWS
VROWS = 144
WIDE = QPH * HD + 128
KEY_AT = 2 * TOK
VALUE_AT = KEY_AT + CACHE
META_AT = VALUE_AT + CACHE
BLOCK_ROWS = META_AT + 16
PLANES = [[z * YC * 8 + i for i in range(YC * 8)] for z in range(Z)]


def seq_permute(value, move):
    pairs = []
    for z in range(Z):
        for y in range(2):
            for c in range(2):
                to_z, to_y, to_c = move(z, y, c)
                pairs.append((z * 4 + y * 2 + c, (to_z % Z) * 4 + to_y * 2 + to_c))
    return lax.ppermute(value, "seq", pairs)


def pack_kernel(length_ref, k_ref, v_ref, nk_ref, nv_ref, out_ref):
    length = length_ref[0]
    out_ref[0:TOK, :] = nk_ref[...]
    out_ref[TOK:KEY_AT, :] = nv_ref[...]
    out_ref[KEY_AT:VALUE_AT, :] = k_ref[0]
    out_ref[VALUE_AT:META_AT, :] = v_ref[0]
    row = lax.broadcasted_iota(jnp.int32, (16, HD), 0)
    meta = jnp.where(row < 8, length // 32, length % 32)
    out_ref[META_AT:BLOCK_ROWS, :] = meta.astype(F32).astype(BF16)


def pack(length, keys, values, new_keys, new_values):
    whole = pl.BlockSpec(memory_space=pltpu.VMEM)
    return pl.pallas_call(
        pack_kernel,
        out_shape=jax.ShapeDtypeStruct((BLOCK_ROWS, HD), BF16),
        in_specs=[pl.BlockSpec(memory_space=pltpu.SMEM)] + [whole] * 4,
        out_specs=whole,
        name="pack",
    )(length, keys, values, new_keys, new_values)


def attention_kernel(shards, first, last, *refs):
    refs = list(refs)
    take = lambda n: [refs.pop(0) for _ in range(n)]
    q_refs, shard_refs = take(BLOCKS), take(shards)
    if not first:
        m_in, acc_in = take(2)
    if last:
        new_refs = take(8)
        ids, span = take(2)
        out_refs = take(BLOCKS)
    m_all, acc = take(2)
    q_all, k_all, v_all, s0, s1, p0, p1, scale0, scale1 = take(9)
    if last:
        new_k, new_v = take(2)
    factor = F32(math.log2(math.e) / math.sqrt(HD))
    for b in range(BLOCKS):
        for h in range(QPH):
            scaled = q_refs[b][:, h * HD : (h + 1) * HD].astype(F32) * factor
            high = scaled.astype(BF16)
            rows = pl.ds(b * ROWS + h * TOK, TOK)
            q_all[rows, 0:HD] = high
            q_all[rows, HD : 2 * HD] = (scaled - high.astype(F32)).astype(BF16)
    if first:
        m_all[...] = jnp.full(m_all.shape, NEG_FILL, F32)
        acc[...] = jnp.zeros(acc.shape, F32)
    else:
        m_all[...] = m_in[...]
        acc[...] = acc_in[...]

    position = lax.broadcasted_iota(jnp.int32, (CACHE, HD), 0)
    lane_position = lax.broadcasted_iota(jnp.int32, (16, CACHE), 1)
    row16 = lax.broadcasted_iota(jnp.int32, (16, CACHE), 0)
    lengths = []
    for ref in shard_refs:
        meta = ref[META_AT:BLOCK_ROWS, :].astype(F32)
        lengths.append(jnp.max(meta[0:8, :] * 32.0 + meta[8:16, :]).astype(jnp.int32))
    total = jnp.int32(0)
    for ref, length in zip(shard_refs, lengths):
        start = pl.multiple_of(total, GRAN)
        counted = position < length
        keys = ref[KEY_AT:VALUE_AT, :]
        keys = jnp.where(counted, keys, jnp.broadcast_to(keys[0:1, :], keys.shape))
        k_all[pl.ds(start, CACHE), 0:HD] = keys
        k_all[pl.ds(start, CACHE), HD : 2 * HD] = keys
        values = ref[VALUE_AT:META_AT, :]
        values = jnp.where(counted, values, jnp.zeros_like(values))
        v_all[0:HD, pl.ds(start, CACHE)] = values.T
        flags = jnp.logical_and(lane_position < length, row16 == 0)
        v_all[HD:VROWS, pl.ds(start, CACHE)] = jnp.where(flags, 1.0, 0.0).astype(BF16)
        total = total + ((length + GRAN - 1) // GRAN) * GRAN
    filler = pl.ds(pl.multiple_of(total, GRAN), CHUNK)
    k_all[filler, :] = jnp.broadcast_to(k_all[0:1, :], (CHUNK, 2 * HD))
    v_all[:, filler] = jnp.zeros((VROWS, CHUNK), BF16)

    left, right = slice(0, TILE), slice(TILE, 2 * TILE)

    def scores(s, k, rows):
        s[...] = lax.dot_general(
            k, q_all[rows, :], (((1,), (1,)), ((), ())), preferred_element_type=F32
        )

    def weigh(s, p, scale, rows):
        before = m_all[:, rows]
        top = jnp.maximum(before, jnp.max(s, axis=0, keepdims=True))
        m_all[:, rows] = top
        p[...] = jnp.exp2(s - top).astype(BF16)
        scale[...] = jnp.exp2(before - top)

    def add(p, scale, v, rows):
        acc[:, rows] = acc[:, rows] * scale[...] + jnp.dot(
            v, p[...], preferred_element_type=F32
        )

    def chunk(i):
        return pl.ds(pl.multiple_of(i * CHUNK, CHUNK), CHUNK)

    count = (total + CHUNK - 1) // CHUNK
    p1[...] = jnp.zeros(p1.shape, BF16)
    scale1[...] = jnp.ones(scale1.shape, F32)
    scores(s0, k_all[0:CHUNK, :], left)

    @pl.loop(0, count)
    def _(i):
        before, here = chunk(jnp.maximum(i - 1, 0)), chunk(i)
        after = chunk(jnp.minimum(i + 1, count - 1))
        scores(s1, k_all[here, :], right)
        weigh(s0[...], p0, scale0, left)
        add(p1, scale1, v_all[:, before], right)
        scores(s0, k_all[after, :], left)
        weigh(s1[...], p1, scale1, right)
        add(p0, scale0, v_all[:, here], left)

    add(p1, scale1, v_all[:, chunk(count - 1)], right)
    if not last:
        return
    for s in range(8):
        rows = pl.ds(s * TOK, TOK)
        fresh = new_refs[s][0:TOK, :]
        new_k[rows, 0:HD] = fresh
        new_k[rows, HD : 2 * HD] = fresh
        new_v[rows, :] = new_refs[s][TOK : 2 * TOK, :]
    ones16 = jnp.where(row16[:, 0:CHUNK] == 0, 1.0, 0.0).astype(BF16)
    values = jnp.concatenate([new_v[...].T, ones16], axis=0)
    scores(s0, new_k[...], left)
    scores(s1, new_k[...], right)

    def rank(i):
        return span[pl.ds(ids[i], 1), :].astype(F32)

    q_rank = jnp.concatenate([rank(b) for b in range(BLOCKS) for _ in range(QPH)], axis=1)
    k_rank = jnp.concatenate([rank(BLOCKS + s) for s in range(8)], axis=0)
    k_rank = jnp.concatenate([k_rank, jnp.zeros((8, HD - TOK), F32)], axis=1).T
    ranks = jnp.concatenate([k_rank[0:TOK, s : s + 1] for s in range(8)], axis=0)
    weigh(jnp.where(ranks <= q_rank[:, left], s0[...], NEG_FILL), p0, scale0, left)
    add(p0, scale0, values, left)
    weigh(jnp.where(ranks <= q_rank[:, right], s1[...], NEG_FILL), p1, scale1, right)
    add(p1, scale1, values, right)
    for b in range(BLOCKS):
        stats = []
        for h in range(QPH):
            cols = slice(b * ROWS + h * TOK, b * ROWS + (h + 1) * TOK)
            held = acc[:, cols]
            weight = held[HD : HD + 1, :]
            out_refs[b][:, h * HD : (h + 1) * HD] = (held[0:HD, :] / weight).T.astype(BF16)
            stats.append(m_all[:, cols] + jnp.log2(weight))
        stats = jnp.concatenate(stats, axis=0)
        high = stats.astype(BF16).astype(F32)
        middle = (stats - high).astype(BF16).astype(F32)
        low = stats - high - middle
        stats = jnp.concatenate([high, middle, low, jnp.zeros((104, TOK), F32)], axis=0)
        out_refs[b][:, QPH * HD : WIDE] = stats.T.astype(BF16)


def attention(q_blocks, shards, state=None, new=None, ids=None, span=None):
    first, last = state is None, new is not None
    m_shape, acc_shape = (1, BLOCKS * ROWS), (VROWS, BLOCKS * ROWS)
    args = [*q_blocks, *shards]
    whole = pl.BlockSpec(memory_space=pltpu.VMEM)
    specs = [whole] * len(args)
    if not first:
        args += state
        specs += [whole] * 2
    keys = len(shards) * CACHE + CHUNK
    scratch = [
        pltpu.VMEM((BLOCKS * ROWS, 2 * HD), BF16),
        pltpu.VMEM((keys, 2 * HD), BF16),
        pltpu.VMEM((VROWS, keys), BF16),
        pltpu.VMEM((CHUNK, TILE), F32),
        pltpu.VMEM((CHUNK, TILE), F32),
        pltpu.VMEM((CHUNK, TILE), BF16),
        pltpu.VMEM((CHUNK, TILE), BF16),
        pltpu.VMEM((1, TILE), F32),
        pltpu.VMEM((1, TILE), F32),
    ]
    if last:
        args += [*new, ids, span]
        specs += [pl.BlockSpec((2 * TOK, HD), lambda i: (0, 0))] * 8
        specs += [pl.BlockSpec(memory_space=pltpu.SMEM), whole]
        out_shape = [jax.ShapeDtypeStruct((TOK, WIDE), BF16)] * BLOCKS
        out_specs = [whole] * BLOCKS
        scratch = [
            pltpu.VMEM(m_shape, F32),
            pltpu.VMEM(acc_shape, F32),
            *scratch,
            pltpu.VMEM((8 * TOK, 2 * HD), BF16),
            pltpu.VMEM((8 * TOK, HD), BF16),
        ]
    else:
        out_shape = [jax.ShapeDtypeStruct(m_shape, F32), jax.ShapeDtypeStruct(acc_shape, F32)]
        out_specs = [whole] * 2
    return pl.pallas_call(
        functools.partial(attention_kernel, len(shards), first, last),
        grid=(1,),
        out_shape=out_shape,
        in_specs=specs,
        out_specs=out_specs,
        scratch_shapes=scratch,
        compiler_params=pltpu.CompilerParams(vmem_limit_bytes=56 * 2**20),
        cost_estimate=pl.CostEstimate(flops=1, bytes_accessed=1, transcendentals=1),
        name="attention",
    )(*args)


def merge_kernel(*refs):
    parts, out_ref = refs[:BLOCKS], refs[BLOCKS]
    stats = []
    for b in range(BLOCKS):
        lanes = parts[b][:, QPH * HD : WIDE].astype(F32)
        stats.append(lanes[:, 0:8] + lanes[:, 8:16] + lanes[:, 16:24])
    top = functools.reduce(jnp.maximum, stats)
    shares = [jnp.exp2(s - top) for s in stats]
    whole = functools.reduce(jnp.add, shares)
    shares = [s / whole for s in shares]
    for h in range(QPH):
        cols = slice(h * HD, (h + 1) * HD)
        out_ref[:, cols] = functools.reduce(
            jnp.add,
            [parts[b][:, cols].astype(F32) * shares[b][:, h : h + 1] for b in range(BLOCKS)],
        ).astype(BF16)


def merge(parts):
    return pl.pallas_call(
        merge_kernel,
        out_shape=jax.ShapeDtypeStruct((TOK, QPH * HD), BF16),
        name="merge",
    )(*parts)


def product_kernel(place_ref, *refs):
    blocks, weights, out_ref, every = refs[:8], refs[8:12], refs[12], refs[13]
    z, yc = place_ref[0], place_ref[1]
    for k in range(Z):
        every[(z + k) % Z] = blocks[k][...]
    rows = every[...].reshape(Z * TOK, QPH * HD)
    for r in range(YC):
        part = jnp.dot(rows, weights[r][...], preferred_element_type=F32)
        out_ref[yc ^ r] = part.astype(BF16).reshape(Z, TOK, 256)


def product(place, blocks, weights):
    whole = pl.BlockSpec(memory_space=pltpu.VMEM)
    return pl.pallas_call(
        product_kernel,
        out_shape=jax.ShapeDtypeStruct((YC, Z, TOK, 256), BF16),
        in_specs=[pl.BlockSpec(memory_space=pltpu.SMEM)] + [whole] * 12,
        out_specs=whole,
        scratch_shapes=[pltpu.VMEM((Z, TOK, QPH * HD), BF16)],
        compiler_params=pltpu.CompilerParams(vmem_limit_bytes=56 * 2**20),
        name="product",
    )(place, *blocks, *weights)


def body(queries, cache_keys, cache_values, new_keys, new_values, cache_len, span_rank, out_weight):
    seq = lax.axis_index("seq")
    z, yc = seq // YC, seq % YC

    own = pack(cache_len, cache_keys, cache_values, new_keys, new_values)
    over_c = lambda v: seq_permute(v, lambda z, y, c: (z, y, 1 - c))
    over_y = lambda v: seq_permute(v, lambda z, y, c: (z, 1 - y, c))
    shift = lambda v, n: seq_permute(v, lambda z, y, c: (z + n, y, c))

    q_far, q_side = shift(queries, 4), over_y(queries)
    own_pair = (own, over_c(own))
    sent, q_far, q_side = lax.optimization_barrier((own, q_far, q_side))
    kv_up, kv_down = shift(sent, -1), shift(sent, 1)
    q_cross = over_y(q_far)
    sent, q_cross = lax.optimization_barrier((own, q_cross))
    kv_two = seq_permute(sent, lambda z, y, c: (z - 2 if z % 2 == 0 else z + 2, y, c))
    q_blocks = (q_cross, q_far, q_side, queries)

    two = jnp.where(z % 2 == 0, z + 2, z + 6)
    row = lambda z, i: z % Z * YC + i
    ids = [row(z + 4, yc ^ 2), row(z + 4, yc), row(z, yc ^ 2), row(z, yc)]
    for n in (z, z + 1, z + 7, two):
        ids += [row(n, yc), row(n, yc ^ 1)]
    ids, span = jnp.stack(ids), span_rank.reshape(Z * YC, TOK)

    ids, span, own = lax.optimization_barrier((ids, span, own))
    own_pair = (own, own_pair[1])
    state = attention(q_blocks, own_pair)
    kv_up, kv_down, *state = lax.optimization_barrier((kv_up, kv_down, *state))
    next_pairs = (kv_up, over_c(kv_up), kv_down, over_c(kv_down))
    weight = lax.optimization_barrier((out_weight, kv_up, kv_down))[0]
    weight_y = over_y(weight)
    weights = [out_weight, over_c(weight), weight_y, over_c(weight_y)]
    state = attention(q_blocks, next_pairs, state)
    kv_two, *state = lax.optimization_barrier((kv_two, *state))
    last_pair = (kv_two, over_c(kv_two))
    new = (*own_pair, *next_pairs, *last_pair)
    cross, far, side, mine = attention(q_blocks, last_pair, state, new, ids, span)
    cross = seq_permute(cross, lambda z, y, c: (z + 4, 1 - y, c))
    attended = merge((cross, shift(far, 4), over_y(side), mine))

    blocks = [attended] + [None] * (Z - 1)
    blocks[1], blocks[7] = shift(attended, -1), shift(attended, 1)
    blocks[2], blocks[6] = shift(attended, -2), shift(attended, 2)
    blocks[3], blocks[5] = shift(blocks[1], -2), shift(blocks[7], 2)
    blocks[4] = shift(blocks[6], 2)
    shares = product(jnp.stack([z, yc]), blocks, weights).reshape(YC * Z, TOK, 256)
    shares = lax.all_to_all(
        shares, ("seq", "head"), 0, 0, axis_index_groups=PLANES, tiled=True
    )
    shares = shares.reshape(YC, Z, TOK, 256).astype(F32)
    return jnp.sum(shares, axis=1).astype(BF16).reshape(YC * TOK, 256)


def solution(mesh):
    return jax.shard_map(
        body,
        mesh=mesh,
        in_specs=(
            P("seq", "head"),
            P("head", "seq", None),
            P("head", "seq", None),
            P("seq", "head"),
            P("seq", "head"),
            P("seq"),
            P(),
            P("head", "seq"),
        ),
        out_specs=P("head", "seq"),
        check_vma=False,
    )
```

```python
import functools
import math

import jax
import jax.numpy as jnp
from jax import lax
from jax.experimental import pallas as pl
from jax.experimental.pallas import tpu as pltpu
from jax.sharding import PartitionSpec as P

NEG_FILL = -1e30
BF16 = jnp.bfloat16
F32 = jnp.float32
Z, YC = 8, 4
QPH, HD = 8, 128
TOK = 64
CACHE = 1024
GRAN = 128
CHUNK = 512
BLOCKS = 4
ROWS = TOK * QPH
TILE = 2 * ROWS
VROWS = 144
WIDE = QPH * HD + 128
KEY_AT = 2 * TOK
VALUE_AT = KEY_AT + CACHE
META_AT = VALUE_AT + CACHE
BLOCK_ROWS = META_AT + 16
PLANES = [[z * YC * 8 + i for i in range(YC * 8)] for z in range(Z)]


def seq_permute(value, move):
    pairs = []
    for z in range(Z):
        for y in range(2):
            for c in range(2):
                to_z, to_y, to_c = move(z, y, c)
                pairs.append((z * 4 + y * 2 + c, (to_z % Z) * 4 + to_y * 2 + to_c))
    return lax.ppermute(value, "seq", pairs)


def pack_kernel(length_ref, k_ref, v_ref, nk_ref, nv_ref, out_ref):
    length = length_ref[0]
    out_ref[0:TOK, :] = nk_ref[...]
    out_ref[TOK:KEY_AT, :] = nv_ref[...]
    out_ref[KEY_AT:VALUE_AT, :] = k_ref[0]
    out_ref[VALUE_AT:META_AT, :] = v_ref[0]
    row = lax.broadcasted_iota(jnp.int32, (16, HD), 0)
    meta = jnp.where(row < 8, length // 32, length % 32)
    out_ref[META_AT:BLOCK_ROWS, :] = meta.astype(F32).astype(BF16)


def pack(length, keys, values, new_keys, new_values):
    whole = pl.BlockSpec(memory_space=pltpu.VMEM)
    return pl.pallas_call(
        pack_kernel,
        out_shape=jax.ShapeDtypeStruct((BLOCK_ROWS, HD), BF16),
        in_specs=[pl.BlockSpec(memory_space=pltpu.SMEM)] + [whole] * 4,
        out_specs=whole,
        name="pack",
    )(length, keys, values, new_keys, new_values)


def attention_kernel(shards, first, last, *refs):
    refs = list(refs)
    take = lambda n: [refs.pop(0) for _ in range(n)]
    q_refs, shard_refs = take(BLOCKS), take(shards)
    if not first:
        m_in, acc_in = take(2)
    if last:
        new_refs = take(8)
        ids, span = take(2)
        out_refs = take(BLOCKS)
    m_all, acc = take(2)
    q_all, k_all, v_all, s0, s1, p0, p1, scale0, scale1 = take(9)
    if last:
        new_k, new_v = take(2)
    factor = F32(math.log2(math.e) / math.sqrt(HD))
    for b in range(BLOCKS):
        for h in range(QPH):
            scaled = q_refs[b][:, h * HD : (h + 1) * HD].astype(F32) * factor
            high = scaled.astype(BF16)
            rows = pl.ds(b * ROWS + h * TOK, TOK)
            q_all[rows, 0:HD] = high
            q_all[rows, HD : 2 * HD] = (scaled - high.astype(F32)).astype(BF16)
    if first:
        m_all[...] = jnp.full(m_all.shape, NEG_FILL, F32)
        acc[...] = jnp.zeros(acc.shape, F32)
    else:
        m_all[...] = m_in[...]
        acc[...] = acc_in[...]

    position = lax.broadcasted_iota(jnp.int32, (CACHE, HD), 0)
    lane_position = lax.broadcasted_iota(jnp.int32, (16, CACHE), 1)
    row16 = lax.broadcasted_iota(jnp.int32, (16, CACHE), 0)
    lengths = []
    for ref in shard_refs:
        meta = ref[META_AT:BLOCK_ROWS, :].astype(F32)
        lengths.append(jnp.max(meta[0:8, :] * 32.0 + meta[8:16, :]).astype(jnp.int32))
    total = jnp.int32(0)
    for ref, length in zip(shard_refs, lengths):
        start = pl.multiple_of(total, GRAN)
        counted = position < length
        keys = ref[KEY_AT:VALUE_AT, :]
        keys = jnp.where(counted, keys, jnp.broadcast_to(keys[0:1, :], keys.shape))
        k_all[pl.ds(start, CACHE), 0:HD] = keys
        k_all[pl.ds(start, CACHE), HD : 2 * HD] = keys
        values = ref[VALUE_AT:META_AT, :]
        values = jnp.where(counted, values, jnp.zeros_like(values))
        v_all[0:HD, pl.ds(start, CACHE)] = values.T
        flags = jnp.logical_and(lane_position < length, row16 == 0)
        v_all[HD:VROWS, pl.ds(start, CACHE)] = jnp.where(flags, 1.0, 0.0).astype(BF16)
        total = total + ((length + GRAN - 1) // GRAN) * GRAN
    filler = pl.ds(pl.multiple_of(total, GRAN), CHUNK)
    k_all[filler, :] = jnp.broadcast_to(k_all[0:1, :], (CHUNK, 2 * HD))
    v_all[:, filler] = jnp.zeros((VROWS, CHUNK), BF16)

    left, right = slice(0, TILE), slice(TILE, 2 * TILE)

    def scores(s, k, rows):
        s[...] = lax.dot_general(
            k, q_all[rows, :], (((1,), (1,)), ((), ())), preferred_element_type=F32
        )

    def weigh(s, p, scale, rows):
        before = m_all[:, rows]
        top = jnp.maximum(before, jnp.max(s, axis=0, keepdims=True))
        m_all[:, rows] = top
        p[...] = jnp.exp2(s - top).astype(BF16)
        scale[...] = jnp.exp2(before - top)

    def add(p, scale, v, rows):
        acc[:, rows] = acc[:, rows] * scale[...] + jnp.dot(
            v, p[...], preferred_element_type=F32
        )

    def chunk(i):
        return pl.ds(pl.multiple_of(i * CHUNK, CHUNK), CHUNK)

    count = (total + CHUNK - 1) // CHUNK
    p1[...] = jnp.zeros(p1.shape, BF16)
    scale1[...] = jnp.ones(scale1.shape, F32)
    scores(s0, k_all[0:CHUNK, :], left)

    @pl.loop(0, count)
    def _(i):
        before, here = chunk(jnp.maximum(i - 1, 0)), chunk(i)
        after = chunk(jnp.minimum(i + 1, count - 1))
        scores(s1, k_all[here, :], right)
        weigh(s0[...], p0, scale0, left)
        add(p1, scale1, v_all[:, before], right)
        scores(s0, k_all[after, :], left)
        weigh(s1[...], p1, scale1, right)
        add(p0, scale0, v_all[:, here], left)

    add(p1, scale1, v_all[:, chunk(count - 1)], right)
    if not last:
        return
    for s in range(8):
        rows = pl.ds(s * TOK, TOK)
        fresh = new_refs[s][0:TOK, :]
        new_k[rows, 0:HD] = fresh
        new_k[rows, HD : 2 * HD] = fresh
        new_v[rows, :] = new_refs[s][TOK : 2 * TOK, :]
    ones16 = jnp.where(row16[:, 0:CHUNK] == 0, 1.0, 0.0).astype(BF16)
    values = jnp.concatenate([new_v[...].T, ones16], axis=0)
    scores(s0, new_k[...], left)
    scores(s1, new_k[...], right)

    def rank(i):
        return span[pl.ds(ids[i], 1), :].astype(F32)

    q_rank = jnp.concatenate([rank(b) for b in range(BLOCKS) for _ in range(QPH)], axis=1)
    k_rank = jnp.concatenate([rank(BLOCKS + s) for s in range(8)], axis=0)
    k_rank = jnp.concatenate([k_rank, jnp.zeros((8, HD - TOK), F32)], axis=1).T
    ranks = jnp.concatenate([k_rank[0:TOK, s : s + 1] for s in range(8)], axis=0)
    weigh(jnp.where(ranks <= q_rank[:, left], s0[...], NEG_FILL), p0, scale0, left)
    add(p0, scale0, values, left)
    weigh(jnp.where(ranks <= q_rank[:, right], s1[...], NEG_FILL), p1, scale1, right)
    add(p1, scale1, values, right)
    for b in range(BLOCKS):
        stats = []
        for h in range(QPH):
            cols = slice(b * ROWS + h * TOK, b * ROWS + (h + 1) * TOK)
            held = acc[:, cols]
            weight = held[HD : HD + 1, :]
            out_refs[b][:, h * HD : (h + 1) * HD] = (held[0:HD, :] / weight).T.astype(BF16)
            stats.append(m_all[:, cols] + jnp.log2(weight))
        stats = jnp.concatenate(stats, axis=0)
        high = stats.astype(BF16).astype(F32)
        middle = (stats - high).astype(BF16).astype(F32)
        low = stats - high - middle
        stats = jnp.concatenate([high, middle, low, jnp.zeros((104, TOK), F32)], axis=0)
        out_refs[b][:, QPH * HD : WIDE] = stats.T.astype(BF16)


def attention(q_blocks, shards, state=None, new=None, ids=None, span=None):
    first, last = state is None, new is not None
    m_shape, acc_shape = (1, BLOCKS * ROWS), (VROWS, BLOCKS * ROWS)
    args = [*q_blocks, *shards]
    whole = pl.BlockSpec(memory_space=pltpu.VMEM)
    specs = [whole] * len(args)
    if not first:
        args += state
        specs += [whole] * 2
    keys = len(shards) * CACHE + CHUNK
    scratch = [
        pltpu.VMEM((BLOCKS * ROWS, 2 * HD), BF16),
        pltpu.VMEM((keys, 2 * HD), BF16),
        pltpu.VMEM((VROWS, keys), BF16),
        pltpu.VMEM((CHUNK, TILE), F32),
        pltpu.VMEM((CHUNK, TILE), F32),
        pltpu.VMEM((CHUNK, TILE), BF16),
        pltpu.VMEM((CHUNK, TILE), BF16),
        pltpu.VMEM((1, TILE), F32),
        pltpu.VMEM((1, TILE), F32),
    ]
    if last:
        args += [*new, ids, span]
        specs += [pl.BlockSpec((2 * TOK, HD), lambda i: (0, 0))] * 8
        specs += [pl.BlockSpec(memory_space=pltpu.SMEM), whole]
        out_shape = [jax.ShapeDtypeStruct((TOK, WIDE), BF16)] * BLOCKS
        out_specs = [whole] * BLOCKS
        scratch = [
            pltpu.VMEM(m_shape, F32),
            pltpu.VMEM(acc_shape, F32),
            *scratch,
            pltpu.VMEM((8 * TOK, 2 * HD), BF16),
            pltpu.VMEM((8 * TOK, HD), BF16),
        ]
    else:
        out_shape = [jax.ShapeDtypeStruct(m_shape, F32), jax.ShapeDtypeStruct(acc_shape, F32)]
        out_specs = [whole] * 2
    return pl.pallas_call(
        functools.partial(attention_kernel, len(shards), first, last),
        grid=(1,),
        out_shape=out_shape,
        in_specs=specs,
        out_specs=out_specs,
        scratch_shapes=scratch,
        compiler_params=pltpu.CompilerParams(vmem_limit_bytes=56 * 2**20),
        cost_estimate=pl.CostEstimate(flops=1, bytes_accessed=1, transcendentals=1),
        name="attention",
    )(*args)


def merge_kernel(*refs):
    parts, out_ref = refs[:BLOCKS], refs[BLOCKS]
    stats = []
    for b in range(BLOCKS):
        lanes = parts[b][:, QPH * HD : WIDE].astype(F32)
        stats.append(lanes[:, 0:8] + lanes[:, 8:16] + lanes[:, 16:24])
    top = functools.reduce(jnp.maximum, stats)
    shares = [jnp.exp2(s - top) for s in stats]
    whole = functools.reduce(jnp.add, shares)
    shares = [s / whole for s in shares]
    for h in range(QPH):
        cols = slice(h * HD, (h + 1) * HD)
        out_ref[:, cols] = functools.reduce(
            jnp.add,
            [parts[b][:, cols].astype(F32) * shares[b][:, h : h + 1] for b in range(BLOCKS)],
        ).astype(BF16)


def merge(parts):
    return pl.pallas_call(
        merge_kernel,
        out_shape=jax.ShapeDtypeStruct((TOK, QPH * HD), BF16),
        name="merge",
    )(*parts)


def product_kernel(place_ref, *refs):
    blocks, weights, out_ref, every = refs[:8], refs[8:12], refs[12], refs[13]
    z, yc = place_ref[0], place_ref[1]
    for k in range(Z):
        every[(z + k) % Z] = blocks[k][...]
    rows = every[...].reshape(Z * TOK, QPH * HD)
    for r in range(YC):
        part = jnp.dot(rows, weights[r][...], preferred_element_type=F32)
        out_ref[yc ^ r] = part.astype(BF16).reshape(Z, TOK, 256)


def product(place, blocks, weights):
    whole = pl.BlockSpec(memory_space=pltpu.VMEM)
    return pl.pallas_call(
        product_kernel,
        out_shape=jax.ShapeDtypeStruct((YC, Z, TOK, 256), BF16),
        in_specs=[pl.BlockSpec(memory_space=pltpu.SMEM)] + [whole] * 12,
        out_specs=whole,
        scratch_shapes=[pltpu.VMEM((Z, TOK, QPH * HD), BF16)],
        compiler_params=pltpu.CompilerParams(vmem_limit_bytes=56 * 2**20),
        name="product",
    )(place, *blocks, *weights)


def body(queries, cache_keys, cache_values, new_keys, new_values, cache_len, span_rank, out_weight):
    seq = lax.axis_index("seq")
    z, yc = seq // YC, seq % YC

    own = pack(cache_len, cache_keys, cache_values, new_keys, new_values)
    over_c = lambda v: seq_permute(v, lambda z, y, c: (z, y, 1 - c))
    over_y = lambda v: seq_permute(v, lambda z, y, c: (z, 1 - y, c))
    shift = lambda v, n: seq_permute(v, lambda z, y, c: (z + n, y, c))

    q_far, q_side = shift(queries, 4), over_y(queries)
    own_pair = (own, over_c(own))
    sent, q_far, q_side = lax.optimization_barrier((own, q_far, q_side))
    kv_up, kv_down = shift(sent, -1), shift(sent, 1)
    q_cross = over_y(q_far)
    sent, q_cross = lax.optimization_barrier((own, q_cross))
    kv_two = seq_permute(sent, lambda z, y, c: (z - 2 if z % 2 == 0 else z + 2, y, c))
    q_blocks = (q_cross, q_far, q_side, queries)

    two = jnp.where(z % 2 == 0, z + 2, z + 6)
    row = lambda z, i: z % Z * YC + i
    ids = [row(z + 4, yc ^ 2), row(z + 4, yc), row(z, yc ^ 2), row(z, yc)]
    for n in (z, z + 1, z + 7, two):
        ids += [row(n, yc), row(n, yc ^ 1)]
    ids, span = jnp.stack(ids), span_rank.reshape(Z * YC, TOK)

    ids, span, own = lax.optimization_barrier((ids, span, own))
    own_pair = (own, own_pair[1])
    state = attention(q_blocks, own_pair)
    kv_up, kv_down, *state = lax.optimization_barrier((kv_up, kv_down, *state))
    next_pairs = (kv_up, over_c(kv_up), kv_down, over_c(kv_down))
    state = attention(q_blocks, next_pairs, state)
    kv_two, weight, *state = lax.optimization_barrier((kv_two, out_weight, *state))
    weight_y = over_y(weight)
    weights = [out_weight, over_c(weight), weight_y, over_c(weight_y)]
    last_pair = (kv_two, over_c(kv_two))
    new = (*own_pair, *next_pairs, *last_pair)
    cross, far, side, mine = attention(q_blocks, last_pair, state, new, ids, span)
    cross = seq_permute(cross, lambda z, y, c: (z + 4, 1 - y, c))
    attended = merge((cross, shift(far, 4), over_y(side), mine))

    blocks = [attended] + [None] * (Z - 1)
    blocks[1], blocks[7] = shift(attended, -1), shift(attended, 1)
    blocks[2], blocks[6] = shift(attended, -2), shift(attended, 2)
    blocks[3], blocks[5] = shift(blocks[1], -2), shift(blocks[7], 2)
    blocks[4] = shift(blocks[6], 2)
    shares = product(jnp.stack([z, yc]), blocks, weights).reshape(YC * Z, TOK, 256)
    shares = lax.all_to_all(
        shares, ("seq", "head"), 0, 0, axis_index_groups=PLANES, tiled=True
    )
    shares = shares.reshape(YC, Z, TOK, 256).astype(F32)
    return jnp.sum(shares, axis=1).astype(BF16).reshape(YC * TOK, 256)


def solution(mesh):
    return jax.shard_map(
        body,
        mesh=mesh,
        in_specs=(
            P("seq", "head"),
            P("head", "seq", None),
            P("head", "seq", None),
            P("seq", "head"),
            P("seq", "head"),
            P("seq"),
            P(),
            P("head", "seq"),
        ),
        out_specs=P("head", "seq"),
        check_vma=False,
    )
```

```python
import functools
import math

import jax
import jax.numpy as jnp
from jax import lax
from jax.experimental import pallas as pl
from jax.experimental.pallas import tpu as pltpu
from jax.sharding import PartitionSpec as P

NEG_FILL = -1e30
BF16 = jnp.bfloat16
F32 = jnp.float32
Z, YC = 8, 4
QPH, HD = 8, 128
TOK = 64
CACHE = 1024
GRAN = 128
CHUNK = 512
BLOCKS = 4
ROWS = TOK * QPH
TILE = 2 * ROWS
VROWS = 144
WIDE = QPH * HD + 128
KEY_AT = 2 * TOK
VALUE_AT = KEY_AT + CACHE
META_AT = VALUE_AT + CACHE
BLOCK_ROWS = META_AT + 16
PLANES = [[z * YC * 8 + i for i in range(YC * 8)] for z in range(Z)]


def seq_permute(value, move):
    pairs = []
    for z in range(Z):
        for y in range(2):
            for c in range(2):
                to_z, to_y, to_c = move(z, y, c)
                pairs.append((z * 4 + y * 2 + c, (to_z % Z) * 4 + to_y * 2 + to_c))
    return lax.ppermute(value, "seq", pairs)


def pack_kernel(length_ref, k_ref, v_ref, nk_ref, nv_ref, out_ref):
    length = length_ref[0]
    out_ref[0:TOK, :] = nk_ref[...]
    out_ref[TOK:KEY_AT, :] = nv_ref[...]
    out_ref[KEY_AT:VALUE_AT, :] = k_ref[0]
    out_ref[VALUE_AT:META_AT, :] = v_ref[0]
    row = lax.broadcasted_iota(jnp.int32, (16, HD), 0)
    meta = jnp.where(row < 8, length // 32, length % 32)
    out_ref[META_AT:BLOCK_ROWS, :] = meta.astype(F32).astype(BF16)


def pack(length, keys, values, new_keys, new_values):
    whole = pl.BlockSpec(memory_space=pltpu.VMEM)
    return pl.pallas_call(
        pack_kernel,
        out_shape=jax.ShapeDtypeStruct((BLOCK_ROWS, HD), BF16),
        in_specs=[pl.BlockSpec(memory_space=pltpu.SMEM)] + [whole] * 4,
        out_specs=whole,
        name="pack",
    )(length, keys, values, new_keys, new_values)


def attention_kernel(shards, first, last, *refs):
    refs = list(refs)
    take = lambda n: [refs.pop(0) for _ in range(n)]
    q_refs, shard_refs = take(BLOCKS), take(shards)
    if not first:
        m_in, acc_in = take(2)
    if last:
        new_refs = take(8)
        ids, span = take(2)
        out_refs = take(BLOCKS)
    m_all, acc = take(2)
    q_all, k_all, v_all, s0, s1, p0, p1, scale0, scale1 = take(9)
    if last:
        new_k, new_v = take(2)
    factor = F32(math.log2(math.e) / math.sqrt(HD))
    for b in range(BLOCKS):
        for h in range(QPH):
            scaled = q_refs[b][:, h * HD : (h + 1) * HD].astype(F32) * factor
            high = scaled.astype(BF16)
            rows = pl.ds(b * ROWS + h * TOK, TOK)
            q_all[rows, 0:HD] = high
            q_all[rows, HD : 2 * HD] = (scaled - high.astype(F32)).astype(BF16)
    if first:
        m_all[...] = jnp.full(m_all.shape, NEG_FILL, F32)
        acc[...] = jnp.zeros(acc.shape, F32)
    else:
        m_all[...] = m_in[...]
        acc[...] = acc_in[...]

    position = lax.broadcasted_iota(jnp.int32, (CACHE, HD), 0)
    lane_position = lax.broadcasted_iota(jnp.int32, (16, CACHE), 1)
    row16 = lax.broadcasted_iota(jnp.int32, (16, CACHE), 0)
    lengths = []
    for ref in shard_refs:
        meta = ref[META_AT:BLOCK_ROWS, :].astype(F32)
        lengths.append(jnp.max(meta[0:8, :] * 32.0 + meta[8:16, :]).astype(jnp.int32))
    total = jnp.int32(0)
    for ref, length in zip(shard_refs, lengths):
        start = pl.multiple_of(total, GRAN)
        counted = position < length
        keys = ref[KEY_AT:VALUE_AT, :]
        keys = jnp.where(counted, keys, jnp.broadcast_to(keys[0:1, :], keys.shape))
        k_all[pl.ds(start, CACHE), 0:HD] = keys
        k_all[pl.ds(start, CACHE), HD : 2 * HD] = keys
        values = ref[VALUE_AT:META_AT, :]
        values = jnp.where(counted, values, jnp.zeros_like(values))
        v_all[0:HD, pl.ds(start, CACHE)] = values.T
        flags = jnp.logical_and(lane_position < length, row16 == 0)
        v_all[HD:VROWS, pl.ds(start, CACHE)] = jnp.where(flags, 1.0, 0.0).astype(BF16)
        total = total + ((length + GRAN - 1) // GRAN) * GRAN
    filler = pl.ds(pl.multiple_of(total, GRAN), CHUNK)
    k_all[filler, :] = jnp.broadcast_to(k_all[0:1, :], (CHUNK, 2 * HD))
    v_all[:, filler] = jnp.zeros((VROWS, CHUNK), BF16)

    left, right = slice(0, TILE), slice(TILE, 2 * TILE)

    def scores(s, k, rows):
        s[...] = lax.dot_general(
            k, q_all[rows, :], (((1,), (1,)), ((), ())), preferred_element_type=F32
        )

    def weigh(s, p, scale, rows):
        before = m_all[:, rows]
        top = jnp.maximum(before, jnp.max(s, axis=0, keepdims=True))
        m_all[:, rows] = top
        p[...] = jnp.exp2(s - top).astype(BF16)
        scale[...] = jnp.exp2(before - top)

    def add(p, scale, v, rows):
        acc[:, rows] = acc[:, rows] * scale[...] + jnp.dot(
            v, p[...], preferred_element_type=F32
        )

    def chunk(i):
        return pl.ds(pl.multiple_of(i * CHUNK, CHUNK), CHUNK)

    count = (total + CHUNK - 1) // CHUNK
    p1[...] = jnp.zeros(p1.shape, BF16)
    scale1[...] = jnp.ones(scale1.shape, F32)
    scores(s0, k_all[0:CHUNK, :], left)

    @pl.loop(0, count)
    def _(i):
        before, here = chunk(jnp.maximum(i - 1, 0)), chunk(i)
        after = chunk(jnp.minimum(i + 1, count - 1))
        scores(s1, k_all[here, :], right)
        weigh(s0[...], p0, scale0, left)
        add(p1, scale1, v_all[:, before], right)
        scores(s0, k_all[after, :], left)
        weigh(s1[...], p1, scale1, right)
        add(p0, scale0, v_all[:, here], left)

    add(p1, scale1, v_all[:, chunk(count - 1)], right)
    if not last:
        return
    for s in range(8):
        rows = pl.ds(s * TOK, TOK)
        fresh = new_refs[s][0:TOK, :]
        new_k[rows, 0:HD] = fresh
        new_k[rows, HD : 2 * HD] = fresh
        new_v[rows, :] = new_refs[s][TOK : 2 * TOK, :]
    ones16 = jnp.where(row16[:, 0:CHUNK] == 0, 1.0, 0.0).astype(BF16)
    values = jnp.concatenate([new_v[...].T, ones16], axis=0)
    scores(s0, new_k[...], left)
    scores(s1, new_k[...], right)

    def rank(i):
        return span[pl.ds(ids[i], 1), :].astype(F32)

    q_rank = jnp.concatenate([rank(b) for b in range(BLOCKS) for _ in range(QPH)], axis=1)
    k_rank = jnp.concatenate([rank(BLOCKS + s) for s in range(8)], axis=0)
    k_rank = jnp.concatenate([k_rank, jnp.zeros((8, HD - TOK), F32)], axis=1).T
    ranks = jnp.concatenate([k_rank[0:TOK, s : s + 1] for s in range(8)], axis=0)
    weigh(jnp.where(ranks <= q_rank[:, left], s0[...], NEG_FILL), p0, scale0, left)
    add(p0, scale0, values, left)
    weigh(jnp.where(ranks <= q_rank[:, right], s1[...], NEG_FILL), p1, scale1, right)
    add(p1, scale1, values, right)
    for b in range(BLOCKS):
        stats = []
        for h in range(QPH):
            cols = slice(b * ROWS + h * TOK, b * ROWS + (h + 1) * TOK)
            held = acc[:, cols]
            weight = held[HD : HD + 1, :]
            out_refs[b][:, h * HD : (h + 1) * HD] = (held[0:HD, :] / weight).T.astype(BF16)
            stats.append(m_all[:, cols] + jnp.log2(weight))
        stats = jnp.concatenate(stats, axis=0)
        high = stats.astype(BF16).astype(F32)
        middle = (stats - high).astype(BF16).astype(F32)
        low = stats - high - middle
        stats = jnp.concatenate([high, middle, low, jnp.zeros((104, TOK), F32)], axis=0)
        out_refs[b][:, QPH * HD : WIDE] = stats.T.astype(BF16)


def attention(q_blocks, shards, state=None, new=None, ids=None, span=None):
    first, last = state is None, new is not None
    m_shape, acc_shape = (1, BLOCKS * ROWS), (VROWS, BLOCKS * ROWS)
    args = [*q_blocks, *shards]
    whole = pl.BlockSpec(memory_space=pltpu.VMEM)
    specs = [whole] * len(args)
    if not first:
        args += state
        specs += [whole] * 2
    keys = len(shards) * CACHE + CHUNK
    scratch = [
        pltpu.VMEM((BLOCKS * ROWS, 2 * HD), BF16),
        pltpu.VMEM((keys, 2 * HD), BF16),
        pltpu.VMEM((VROWS, keys), BF16),
        pltpu.VMEM((CHUNK, TILE), F32),
        pltpu.VMEM((CHUNK, TILE), F32),
        pltpu.VMEM((CHUNK, TILE), BF16),
        pltpu.VMEM((CHUNK, TILE), BF16),
        pltpu.VMEM((1, TILE), F32),
        pltpu.VMEM((1, TILE), F32),
    ]
    if last:
        args += [*new, ids, span]
        specs += [pl.BlockSpec((2 * TOK, HD), lambda i: (0, 0))] * 8
        specs += [pl.BlockSpec(memory_space=pltpu.SMEM), whole]
        out_shape = [jax.ShapeDtypeStruct((TOK, WIDE), BF16)] * BLOCKS
        out_specs = [whole] * BLOCKS
        scratch = [
            pltpu.VMEM(m_shape, F32),
            pltpu.VMEM(acc_shape, F32),
            *scratch,
            pltpu.VMEM((8 * TOK, 2 * HD), BF16),
            pltpu.VMEM((8 * TOK, HD), BF16),
        ]
    else:
        out_shape = [jax.ShapeDtypeStruct(m_shape, F32), jax.ShapeDtypeStruct(acc_shape, F32)]
        out_specs = [whole] * 2
    return pl.pallas_call(
        functools.partial(attention_kernel, len(shards), first, last),
        grid=(1,),
        out_shape=out_shape,
        in_specs=specs,
        out_specs=out_specs,
        scratch_shapes=scratch,
        compiler_params=pltpu.CompilerParams(vmem_limit_bytes=56 * 2**20),
        cost_estimate=pl.CostEstimate(flops=1, bytes_accessed=1, transcendentals=1),
        name="attention",
    )(*args)


def merge_kernel(*refs):
    parts, out_ref = refs[:BLOCKS], refs[BLOCKS]
    stats = []
    for b in range(BLOCKS):
        lanes = parts[b][:, QPH * HD : WIDE].astype(F32)
        stats.append(lanes[:, 0:8] + lanes[:, 8:16] + lanes[:, 16:24])
    top = functools.reduce(jnp.maximum, stats)
    shares = [jnp.exp2(s - top) for s in stats]
    whole = functools.reduce(jnp.add, shares)
    shares = [s / whole for s in shares]
    for h in range(QPH):
        cols = slice(h * HD, (h + 1) * HD)
        out_ref[:, cols] = functools.reduce(
            jnp.add,
            [parts[b][:, cols].astype(F32) * shares[b][:, h : h + 1] for b in range(BLOCKS)],
        ).astype(BF16)


def merge(parts):
    return pl.pallas_call(
        merge_kernel,
        out_shape=jax.ShapeDtypeStruct((TOK, QPH * HD), BF16),
        name="merge",
    )(*parts)


def product_kernel(place_ref, *refs):
    blocks, weights, out_ref, every = refs[:8], refs[8:12], refs[12], refs[13]
    z, yc = place_ref[0], place_ref[1]
    for k in range(Z):
        every[(z + k) % Z] = blocks[k][...]
    rows = every[...].reshape(Z * TOK, QPH * HD)
    for r in range(YC):
        part = jnp.dot(rows, weights[r][...], preferred_element_type=F32)
        out_ref[yc ^ r] = part.astype(BF16).reshape(Z, TOK, 256)


def product(place, blocks, weights):
    whole = pl.BlockSpec(memory_space=pltpu.VMEM)
    return pl.pallas_call(
        product_kernel,
        out_shape=jax.ShapeDtypeStruct((YC, Z, TOK, 256), BF16),
        in_specs=[pl.BlockSpec(memory_space=pltpu.SMEM)] + [whole] * 12,
        out_specs=whole,
        scratch_shapes=[pltpu.VMEM((Z, TOK, QPH * HD), BF16)],
        compiler_params=pltpu.CompilerParams(vmem_limit_bytes=56 * 2**20),
        name="product",
    )(place, *blocks, *weights)


def body(queries, cache_keys, cache_values, new_keys, new_values, cache_len, span_rank, out_weight):
    seq = lax.axis_index("seq")
    z, yc = seq // YC, seq % YC

    own = pack(cache_len, cache_keys, cache_values, new_keys, new_values)
    over_c = lambda v: seq_permute(v, lambda z, y, c: (z, y, 1 - c))
    over_y = lambda v: seq_permute(v, lambda z, y, c: (z, 1 - y, c))
    shift = lambda v, n: seq_permute(v, lambda z, y, c: (z + n, y, c))

    q_far, q_side = shift(queries, 4), over_y(queries)
    own_pair = (own, over_c(own))
    sent, q_far, q_side = lax.optimization_barrier((own, q_far, q_side))
    kv_up, kv_down = shift(sent, -1), shift(sent, 1)
    q_cross = over_y(q_far)
    sent, q_cross = lax.optimization_barrier((own, q_cross))
    kv_two = seq_permute(sent, lambda z, y, c: (z - 2 if z % 2 == 0 else z + 2, y, c))
    q_blocks = (q_cross, q_far, q_side, queries)

    two = jnp.where(z % 2 == 0, z + 2, z + 6)
    row = lambda z, i: z % Z * YC + i
    ids = [row(z + 4, yc ^ 2), row(z + 4, yc), row(z, yc ^ 2), row(z, yc)]
    for n in (z, z + 1, z + 7, two):
        ids += [row(n, yc), row(n, yc ^ 1)]
    ids, span = jnp.stack(ids), span_rank.reshape(Z * YC, TOK)

    ids, span, own = lax.optimization_barrier((ids, span, own))
    own_pair = (own, own_pair[1])
    state = attention(q_blocks, own_pair)
    kv_up, kv_down, *state = lax.optimization_barrier((kv_up, kv_down, *state))
    next_pairs = (kv_up, over_c(kv_up), kv_down, over_c(kv_down))
    state = attention(q_blocks, next_pairs, state)
    kv_two, weight, *state = lax.optimization_barrier((kv_two, out_weight, *state))
    weight_y = over_y(weight)
    weight_c = over_c(weight)
    last_pair = (kv_two, over_c(kv_two))
    new = (*own_pair, *next_pairs, *last_pair)
    cross, far, side, mine = attention(q_blocks, last_pair, state, new, ids, span)
    weight_y, cross, far, side, mine = lax.optimization_barrier(
        (weight_y, cross, far, side, mine)
    )
    weights = [out_weight, weight_c, weight_y, over_c(weight_y)]
    cross = seq_permute(cross, lambda z, y, c: (z + 4, 1 - y, c))
    attended = merge((cross, shift(far, 4), over_y(side), mine))

    blocks = [attended] + [None] * (Z - 1)
    for k in (1, 2, 3):
        blocks[k] = shift(blocks[k - 1], -1)
        blocks[Z - k] = shift(blocks[(Z - k + 1) % Z], 1)
    blocks[4] = shift(blocks[3], -1)
    shares = product(jnp.stack([z, yc]), blocks, weights).reshape(YC * Z, TOK, 256)
    shares = lax.all_to_all(
        shares, ("seq", "head"), 0, 0, axis_index_groups=PLANES, tiled=True
    )
    shares = shares.reshape(YC, Z, TOK, 256).astype(F32)
    return jnp.sum(shares, axis=1).astype(BF16).reshape(YC * TOK, 256)


def solution(mesh):
    return jax.shard_map(
        body,
        mesh=mesh,
        in_specs=(
            P("seq", "head"),
            P("head", "seq", None),
            P("head", "seq", None),
            P("seq", "head"),
            P("seq", "head"),
            P("seq"),
            P(),
            P("head", "seq"),
        ),
        out_specs=P("head", "seq"),
        check_vma=False,
    )
```

```python
import functools
import math

import jax
import jax.numpy as jnp
from jax import lax
from jax.experimental import pallas as pl
from jax.experimental.pallas import tpu as pltpu
from jax.sharding import PartitionSpec as P

NEG_FILL = -1e30
BF16 = jnp.bfloat16
F32 = jnp.float32
Z, YC = 8, 4
QPH, HD = 8, 128
TOK = 64
CACHE = 1024
GRAN = 128
CHUNK = 512
BLOCKS = 4
ROWS = TOK * QPH
TILE = 2 * ROWS
VROWS = 144
WIDE = QPH * HD + 128
KEY_AT = 2 * TOK
VALUE_AT = KEY_AT + CACHE
META_AT = VALUE_AT + CACHE
BLOCK_ROWS = META_AT + 16
PLANES = [[z * YC * 8 + i for i in range(YC * 8)] for z in range(Z)]


def seq_permute(value, move):
    pairs = []
    for z in range(Z):
        for y in range(2):
            for c in range(2):
                to_z, to_y, to_c = move(z, y, c)
                pairs.append((z * 4 + y * 2 + c, (to_z % Z) * 4 + to_y * 2 + to_c))
    return lax.ppermute(value, "seq", pairs)


def pack_kernel(length_ref, k_ref, v_ref, nk_ref, nv_ref, out_ref):
    length = length_ref[0]
    out_ref[0:TOK, :] = nk_ref[...]
    out_ref[TOK:KEY_AT, :] = nv_ref[...]
    out_ref[KEY_AT:VALUE_AT, :] = k_ref[0]
    out_ref[VALUE_AT:META_AT, :] = v_ref[0]
    row = lax.broadcasted_iota(jnp.int32, (16, HD), 0)
    meta = jnp.where(row < 8, length // 32, length % 32)
    out_ref[META_AT:BLOCK_ROWS, :] = meta.astype(F32).astype(BF16)


def pack(length, keys, values, new_keys, new_values):
    whole = pl.BlockSpec(memory_space=pltpu.VMEM)
    return pl.pallas_call(
        pack_kernel,
        out_shape=jax.ShapeDtypeStruct((BLOCK_ROWS, HD), BF16),
        in_specs=[pl.BlockSpec(memory_space=pltpu.SMEM)] + [whole] * 4,
        out_specs=whole,
        name="pack",
    )(length, keys, values, new_keys, new_values)


def attention_kernel(shards, first, last, *refs):
    refs = list(refs)
    take = lambda n: [refs.pop(0) for _ in range(n)]
    q_refs, shard_refs = take(BLOCKS), take(shards)
    if not first:
        m_in, acc_in = take(2)
    if last:
        new_refs = take(8)
        ids, span = take(2)
        out_refs = take(BLOCKS)
    m_all, acc = take(2)
    q_all, k_all, v_all, s0, s1, p0, p1, scale0, scale1 = take(9)
    if last:
        new_k, new_v = take(2)
    factor = F32(math.log2(math.e) / math.sqrt(HD))
    for b in range(BLOCKS):
        for h in range(QPH):
            scaled = q_refs[b][:, h * HD : (h + 1) * HD].astype(F32) * factor
            high = scaled.astype(BF16)
            rows = pl.ds(b * ROWS + h * TOK, TOK)
            q_all[rows, 0:HD] = high
            q_all[rows, HD : 2 * HD] = (scaled - high.astype(F32)).astype(BF16)
    if first:
        m_all[...] = jnp.full(m_all.shape, NEG_FILL, F32)
        acc[...] = jnp.zeros(acc.shape, F32)
    else:
        m_all[...] = m_in[...]
        acc[...] = acc_in[...]

    position = lax.broadcasted_iota(jnp.int32, (CACHE, HD), 0)
    lane_position = lax.broadcasted_iota(jnp.int32, (16, CACHE), 1)
    row16 = lax.broadcasted_iota(jnp.int32, (16, CACHE), 0)
    lengths = []
    for ref in shard_refs:
        meta = ref[META_AT:BLOCK_ROWS, :].astype(F32)
        lengths.append(jnp.max(meta[0:8, :] * 32.0 + meta[8:16, :]).astype(jnp.int32))
    total = jnp.int32(0)
    for ref, length in zip(shard_refs, lengths):
        start = pl.multiple_of(total, GRAN)
        counted = position < length
        keys = ref[KEY_AT:VALUE_AT, :]
        keys = jnp.where(counted, keys, jnp.broadcast_to(keys[0:1, :], keys.shape))
        k_all[pl.ds(start, CACHE), 0:HD] = keys
        k_all[pl.ds(start, CACHE), HD : 2 * HD] = keys
        values = ref[VALUE_AT:META_AT, :]
        values = jnp.where(counted, values, jnp.zeros_like(values))
        v_all[0:HD, pl.ds(start, CACHE)] = values.T
        flags = jnp.logical_and(lane_position < length, row16 == 0)
        v_all[HD:VROWS, pl.ds(start, CACHE)] = jnp.where(flags, 1.0, 0.0).astype(BF16)
        total = total + ((length + GRAN - 1) // GRAN) * GRAN
    filler = pl.ds(pl.multiple_of(total, GRAN), CHUNK)
    k_all[filler, :] = jnp.broadcast_to(k_all[0:1, :], (CHUNK, 2 * HD))
    v_all[:, filler] = jnp.zeros((VROWS, CHUNK), BF16)

    left, right = slice(0, TILE), slice(TILE, 2 * TILE)

    def scores(s, k, rows):
        s[...] = lax.dot_general(
            k, q_all[rows, :], (((1,), (1,)), ((), ())), preferred_element_type=F32
        )

    def weigh(s, p, scale, rows):
        before = m_all[:, rows]
        top = jnp.maximum(before, jnp.max(s, axis=0, keepdims=True))
        m_all[:, rows] = top
        p[...] = jnp.exp2(s - top).astype(BF16)
        scale[...] = jnp.exp2(before - top)

    def add(p, scale, v, rows):
        acc[:, rows] = acc[:, rows] * scale[...] + jnp.dot(
            v, p[...], preferred_element_type=F32
        )

    def chunk(i):
        return pl.ds(pl.multiple_of(i * CHUNK, CHUNK), CHUNK)

    count = (total + CHUNK - 1) // CHUNK
    p1[...] = jnp.zeros(p1.shape, BF16)
    scale1[...] = jnp.ones(scale1.shape, F32)
    scores(s0, k_all[0:CHUNK, :], left)

    @pl.loop(0, count)
    def _(i):
        before, here = chunk(jnp.maximum(i - 1, 0)), chunk(i)
        after = chunk(jnp.minimum(i + 1, count - 1))
        scores(s1, k_all[here, :], right)
        weigh(s0[...], p0, scale0, left)
        add(p1, scale1, v_all[:, before], right)
        scores(s0, k_all[after, :], left)
        weigh(s1[...], p1, scale1, right)
        add(p0, scale0, v_all[:, here], left)

    add(p1, scale1, v_all[:, chunk(count - 1)], right)
    if not last:
        return
    for s in range(8):
        rows = pl.ds(s * TOK, TOK)
        fresh = new_refs[s][0:TOK, :]
        new_k[rows, 0:HD] = fresh
        new_k[rows, HD : 2 * HD] = fresh
        new_v[rows, :] = new_refs[s][TOK : 2 * TOK, :]
    ones16 = jnp.where(row16[:, 0:CHUNK] == 0, 1.0, 0.0).astype(BF16)
    values = jnp.concatenate([new_v[...].T, ones16], axis=0)
    scores(s0, new_k[...], left)
    scores(s1, new_k[...], right)

    def rank(i):
        return span[pl.ds(ids[i], 1), :].astype(F32)

    q_rank = jnp.concatenate([rank(b) for b in range(BLOCKS) for _ in range(QPH)], axis=1)
    k_rank = jnp.concatenate([rank(BLOCKS + s) for s in range(8)], axis=0)
    k_rank = jnp.concatenate([k_rank, jnp.zeros((8, HD - TOK), F32)], axis=1).T
    ranks = jnp.concatenate([k_rank[0:TOK, s : s + 1] for s in range(8)], axis=0)
    weigh(jnp.where(ranks <= q_rank[:, left], s0[...], NEG_FILL), p0, scale0, left)
    add(p0, scale0, values, left)
    weigh(jnp.where(ranks <= q_rank[:, right], s1[...], NEG_FILL), p1, scale1, right)
    add(p1, scale1, values, right)
    for b in range(BLOCKS):
        stats = []
        for h in range(QPH):
            cols = slice(b * ROWS + h * TOK, b * ROWS + (h + 1) * TOK)
            held = acc[:, cols]
            weight = held[HD : HD + 1, :]
            out_refs[b][:, h * HD : (h + 1) * HD] = (held[0:HD, :] / weight).T.astype(BF16)
            stats.append(m_all[:, cols] + jnp.log2(weight))
        stats = jnp.concatenate(stats, axis=0)
        high = stats.astype(BF16).astype(F32)
        middle = (stats - high).astype(BF16).astype(F32)
        low = stats - high - middle
        stats = jnp.concatenate([high, middle, low, jnp.zeros((104, TOK), F32)], axis=0)
        out_refs[b][:, QPH * HD : WIDE] = stats.T.astype(BF16)


def attention(q_blocks, shards, state=None, new=None, ids=None, span=None):
    first, last = state is None, new is not None
    m_shape, acc_shape = (1, BLOCKS * ROWS), (VROWS, BLOCKS * ROWS)
    args = [*q_blocks, *shards]
    whole = pl.BlockSpec(memory_space=pltpu.VMEM)
    specs = [whole] * len(args)
    if not first:
        args += state
        specs += [whole] * 2
    keys = len(shards) * CACHE + CHUNK
    scratch = [
        pltpu.VMEM((BLOCKS * ROWS, 2 * HD), BF16),
        pltpu.VMEM((keys, 2 * HD), BF16),
        pltpu.VMEM((VROWS, keys), BF16),
        pltpu.VMEM((CHUNK, TILE), F32),
        pltpu.VMEM((CHUNK, TILE), F32),
        pltpu.VMEM((CHUNK, TILE), BF16),
        pltpu.VMEM((CHUNK, TILE), BF16),
        pltpu.VMEM((1, TILE), F32),
        pltpu.VMEM((1, TILE), F32),
    ]
    if last:
        args += [*new, ids, span]
        specs += [pl.BlockSpec((2 * TOK, HD), lambda i: (0, 0))] * 8
        specs += [pl.BlockSpec(memory_space=pltpu.SMEM), whole]
        out_shape = [jax.ShapeDtypeStruct((TOK, WIDE), BF16)] * BLOCKS
        out_specs = [whole] * BLOCKS
        scratch = [
            pltpu.VMEM(m_shape, F32),
            pltpu.VMEM(acc_shape, F32),
            *scratch,
            pltpu.VMEM((8 * TOK, 2 * HD), BF16),
            pltpu.VMEM((8 * TOK, HD), BF16),
        ]
    else:
        out_shape = [jax.ShapeDtypeStruct(m_shape, F32), jax.ShapeDtypeStruct(acc_shape, F32)]
        out_specs = [whole] * 2
    return pl.pallas_call(
        functools.partial(attention_kernel, len(shards), first, last),
        grid=(1,),
        out_shape=out_shape,
        in_specs=specs,
        out_specs=out_specs,
        scratch_shapes=scratch,
        compiler_params=pltpu.CompilerParams(vmem_limit_bytes=56 * 2**20),
        cost_estimate=pl.CostEstimate(flops=1, bytes_accessed=1, transcendentals=1),
        name="attention",
    )(*args)


def merge_kernel(*refs):
    parts, out_ref = refs[:BLOCKS], refs[BLOCKS]
    stats = []
    for b in range(BLOCKS):
        lanes = parts[b][:, QPH * HD : WIDE].astype(F32)
        stats.append(lanes[:, 0:8] + lanes[:, 8:16] + lanes[:, 16:24])
    top = functools.reduce(jnp.maximum, stats)
    shares = [jnp.exp2(s - top) for s in stats]
    whole = functools.reduce(jnp.add, shares)
    shares = [s / whole for s in shares]
    for h in range(QPH):
        cols = slice(h * HD, (h + 1) * HD)
        out_ref[:, cols] = functools.reduce(
            jnp.add,
            [parts[b][:, cols].astype(F32) * shares[b][:, h : h + 1] for b in range(BLOCKS)],
        ).astype(BF16)


def merge(parts):
    return pl.pallas_call(
        merge_kernel,
        out_shape=jax.ShapeDtypeStruct((TOK, QPH * HD), BF16),
        name="merge",
    )(*parts)


def product_kernel(place_ref, *refs):
    blocks, weights, out_ref, every = refs[:8], refs[8:12], refs[12], refs[13]
    z, yc = place_ref[0], place_ref[1]
    for k in range(Z):
        every[(z + k) % Z] = blocks[k][...]
    rows = every[...].reshape(Z * TOK, QPH * HD)
    for r in range(YC):
        part = jnp.dot(rows, weights[r][...], preferred_element_type=F32)
        out_ref[yc ^ r] = part.astype(BF16).reshape(Z, TOK, 256)


def product(place, blocks, weights):
    whole = pl.BlockSpec(memory_space=pltpu.VMEM)
    return pl.pallas_call(
        product_kernel,
        out_shape=jax.ShapeDtypeStruct((YC, Z, TOK, 256), BF16),
        in_specs=[pl.BlockSpec(memory_space=pltpu.SMEM)] + [whole] * 12,
        out_specs=whole,
        scratch_shapes=[pltpu.VMEM((Z, TOK, QPH * HD), BF16)],
        compiler_params=pltpu.CompilerParams(vmem_limit_bytes=56 * 2**20),
        name="product",
    )(place, *blocks, *weights)


def body(queries, cache_keys, cache_values, new_keys, new_values, cache_len, span_rank, out_weight):
    seq = lax.axis_index("seq")
    z, yc = seq // YC, seq % YC

    own = pack(cache_len, cache_keys, cache_values, new_keys, new_values)
    over_c = lambda v: seq_permute(v, lambda z, y, c: (z, y, 1 - c))
    over_y = lambda v: seq_permute(v, lambda z, y, c: (z, 1 - y, c))
    shift = lambda v, n: seq_permute(v, lambda z, y, c: (z + n, y, c))

    q_far, q_side = shift(queries, 4), over_y(queries)
    own_pair = (own, over_c(own))
    sent, q_far, q_side = lax.optimization_barrier((own, q_far, q_side))
    kv_up, kv_down = shift(sent, -1), shift(sent, 1)
    q_cross = over_y(q_far)
    sent, q_cross = lax.optimization_barrier((own, q_cross))
    kv_two = seq_permute(sent, lambda z, y, c: (z - 2 if z % 2 == 0 else z + 2, y, c))
    q_blocks = (q_cross, q_far, q_side, queries)

    two = jnp.where(z % 2 == 0, z + 2, z + 6)
    row = lambda z, i: z % Z * YC + i
    ids = [row(z + 4, yc ^ 2), row(z + 4, yc), row(z, yc ^ 2), row(z, yc)]
    for n in (z, z + 1, z + 7, two):
        ids += [row(n, yc), row(n, yc ^ 1)]
    ids, span = jnp.stack(ids), span_rank.reshape(Z * YC, TOK)

    place = jnp.stack([z, yc])
    place, ids, span, own = lax.optimization_barrier((place, ids, span, own))
    own_pair = (own, own_pair[1])
    state = attention(q_blocks, own_pair)
    kv_up, kv_down, *state = lax.optimization_barrier((kv_up, kv_down, *state))
    next_pairs = (kv_up, over_c(kv_up), kv_down, over_c(kv_down))
    state = attention(q_blocks, next_pairs, state)
    kv_two, weight, *state = lax.optimization_barrier((kv_two, out_weight, *state))
    weight_y = over_y(weight)
    weight_c = over_c(weight)
    last_pair = (kv_two, over_c(kv_two))
    new = (*own_pair, *next_pairs, *last_pair)
    cross, far, side, mine = attention(q_blocks, last_pair, state, new, ids, span)
    weight_y, cross, far, side, mine = lax.optimization_barrier(
        (weight_y, cross, far, side, mine)
    )
    weight_yc = over_c(weight_y)
    cross = seq_permute(cross, lambda z, y, c: (z + 4, 1 - y, c))
    parts = (cross, shift(far, 4), over_y(side), mine)
    weight_c, weight_yc, *parts = lax.optimization_barrier((weight_c, weight_yc, *parts))
    weights = [out_weight, weight_c, weight_y, weight_yc]
    attended = merge(parts)

    blocks = [attended] + [None] * (Z - 1)
    for k in (1, 2, 3):
        blocks[k] = shift(blocks[k - 1], -1)
        blocks[Z - k] = shift(blocks[(Z - k + 1) % Z], 1)
    blocks[4] = shift(blocks[3], -1)
    shares = product(place, blocks, weights).reshape(YC * Z, TOK, 256)
    shares = lax.all_to_all(
        shares, ("seq", "head"), 0, 0, axis_index_groups=PLANES, tiled=True
    )
    shares = shares.reshape(YC, Z, TOK, 256).astype(F32)
    return jnp.sum(shares, axis=1).astype(BF16).reshape(YC * TOK, 256)


def solution(mesh):
    return jax.shard_map(
        body,
        mesh=mesh,
        in_specs=(
            P("seq", "head"),
            P("head", "seq", None),
            P("head", "seq", None),
            P("seq", "head"),
            P("seq", "head"),
            P("seq"),
            P(),
            P("head", "seq"),
        ),
        out_specs=P("head", "seq"),
        check_vma=False,
    )
```
